128 devices in a mesh: lat: 4 (over x), tok: 32 (over y, z, core).
Axes of the slice: x: 4, y: 4, z: 4, core: 2. Of those that a mesh axis runs over, the one named last changes fastest.
Arguments:
- tokens: bfloat16 [65536, 512], P('tok'), may hold values from -60 to 60
- date_index: int32 [65536], P('tok'), may hold values from 0 to 1
- valid: int32 [65536], P('tok'), may hold values from 0 to 1, as said below
- date_table: float32 [2, 512], replicated, may hold values from -6 to 6
- latents: bfloat16 [1024, 512], replicated, may hold values from -60 to 60
- wq_enc: bfloat16 [512, 512], P(None, 'lat'), may hold values from -1 to 1
- wk_enc: bfloat16 [512, 512], P(None, 'lat'), may hold values from -1 to 1
- wv_enc: bfloat16 [512, 512], P(None, 'lat'), may hold values from -0.25 to 0.25
- wo_enc: bfloat16 [512, 512], replicated, may hold values from -0.25 to 0.25
- w_lat_up: bfloat16 [512, 2048], replicated, may hold values from -0.25 to 0.25
- w_lat_down: bfloat16 [2048, 512], replicated, may hold values from -0.125 to 0.125
- wq_dec: bfloat16 [512, 512], replicated, may hold values from -1 to 1
- wk_dec: bfloat16 [512, 512], replicated, may hold values from -1 to 1
- wv_dec: bfloat16 [512, 512], replicated, may hold values from -0.25 to 0.25
- wo_dec: bfloat16 [512, 512], replicated, may hold values from -0.25 to 0.25
- w_out_up: bfloat16 [512, 2048], replicated, may hold values from -0.25 to 0.25
- w_out_down: bfloat16 [2048, 128], replicated, may hold values from -0.125 to 0.125
Outputs:
- change: float32 [65536, 128], P(('tok', 'lat'))
The draws below stay inside these ranges and needn't reach their ends.
Inputs may be any that keep to these rules, and one draw needn't show every extreme that they name: `valid`: the first token of every aligned block of 16 tokens is usable.
All inputs are finite; a program needn't handle non-finite values.
Results may differ from the reference program's by a relative error of at most 0.028.
The reference program's roundings to bfloat16 on the way count: a program that leaves them out, or rounds other values in their place, can miss the bound.
Values may be sent and summed in bfloat16 or wider, within the bound.
No kernel may reach another device: no remote copies, remote signals or barrier semaphores. Data moves between devices by JAX's collectives and lax.ppermute only.
A program may use at most 128 MiB of HBM per device.

```python
import jax
import jax.numpy as jnp
from jax import lax

D = 512
HEADS = 8
L = 1024
F_LAT = 2048
FD = 2048
C = 128
TOK_DEV = 2048
TOKENS = 65536


def shared_matrix(key, salt):
    return jax.random.normal(jax.random.fold_in(key, salt), (D, D), jnp.float32) * D ** (-0.5)


def drawn_rows(key, count):
    standard = jax.random.normal(jax.random.fold_in(key, 11), (count, D), jnp.float32)
    result = standard
    return jnp.clip(result, -60.0, 60.0)


def draw_tokens(key, part):
    key = jax.random.fold_in(key, 1)
    return drawn_rows(key, TOKENS).astype(jnp.bfloat16)


def draw_latents(key, part):
    key = jax.random.fold_in(key, 2)
    return drawn_rows(key, L).astype(jnp.bfloat16)


def query_matrix(key, salt):
    return jnp.clip(shared_matrix(key, salt), -1.0, 1.0).astype(jnp.bfloat16)


def draw_wq_enc(key, part):
    return query_matrix(key, 901)


def draw_wk_enc(key, part):
    key = jax.random.fold_in(key, 4)
    private = jax.random.normal(key, (D, D), jnp.float32) * D ** (-0.5)
    result = private
    return jnp.clip(result, -1.0, 1.0).astype(jnp.bfloat16)


def draw_wq_dec(key, part):
    return query_matrix(key, 902)


def draw_wk_dec(key, part):
    key = jax.random.fold_in(key, 6)
    private = jax.random.normal(key, (D, D), jnp.float32) * D ** (-0.5)
    result = private
    return jnp.clip(result, -1.0, 1.0).astype(jnp.bfloat16)


def draw_valid(key, part):
    key = jax.random.fold_in(key, 7)
    flags = jax.random.randint(key, (TOKENS,), 0, 4) > 0
    leading = jnp.arange(TOKENS) % 16 == 0
    return jnp.where(flags | leading, 1, 0).astype(jnp.int32)


def touch_ends(array, own_key, low, largest):
    spot = [jax.random.randint(jax.random.fold_in(own_key, axis), (), 0, length) for axis, length in enumerate(array.shape)]
    main_axis = array.shape.index(max(array.shape))
    neighbour = spot[:main_axis] + [(spot[main_axis] + 1) % array.shape[main_axis]] + spot[main_axis + 1:]
    return array.at[tuple(spot)].set(low).at[tuple(neighbour)].set(largest)


def block_levels(stream_key, shape, split, least, largest):
    loudness, own = 1.0, jax.random.fold_in(stream_key, 6)
    for position, shards_of in split:
        steps = jnp.exp(jax.random.uniform(jax.random.fold_in(own, position), (shards_of,), jnp.float32, least / len(split), largest / len(split)))
        loudness = loudness * jnp.repeat(steps, shape[position] // shards_of).reshape([-1 if axis == position else 1 for axis in range(len(shape))])
    return loudness


def gaussian(own_key, shape, width, most, shards=(), held_as=jnp.bfloat16):
    entries = jax.random.normal(own_key, shape, jnp.float32) * width
    if len(shards) > 0:
        entries = block_levels(own_key, shape, shards, -0.22, 0.18) * entries
    return jnp.clip(entries, min=-most, max=most).astype(held_as)


def setup_inputs(seed: int = 0) -> dict:
    streams_of = jax.random.split(jax.random.key(seed), 18)
    tokens = draw_tokens(jax.random.fold_in(streams_of[17], 71), 0)
    date_index = touch_ends(jax.random.randint(streams_of[1], (TOKENS,), 0, 2), jax.random.fold_in(streams_of[1], 1), 0, 1).astype(jnp.int32)
    valid = draw_valid(jax.random.fold_in(streams_of[17], 71), 0)
    date_table = gaussian(streams_of[3], (2, D), 1.0, 6.0, (), jnp.float32)
    latents = draw_latents(jax.random.fold_in(streams_of[17], 71), 0)
    wq_enc = draw_wq_enc(jax.random.fold_in(streams_of[17], 71), 0)
    wk_enc = draw_wk_enc(jax.random.fold_in(streams_of[17], 71), 0)
    wv_enc = gaussian(streams_of[7], (D, D), D ** -0.5, 0.25, ((1, 4),))
    wo_enc = gaussian(streams_of[8], (D, D), D ** -0.5, 0.25)
    w_lat_up = gaussian(streams_of[9], (D, F_LAT), D ** -0.5, 0.25)
    w_lat_down = gaussian(streams_of[10], (F_LAT, D), F_LAT ** -0.5, 0.125)
    wq_dec = draw_wq_dec(jax.random.fold_in(streams_of[17], 71), 0)
    wk_dec = draw_wk_dec(jax.random.fold_in(streams_of[17], 71), 0)
    wv_dec = gaussian(streams_of[13], (D, D), D ** -0.5, 0.25)
    wo_dec = gaussian(streams_of[14], (D, D), D ** -0.5, 0.25)
    w_out_up = gaussian(streams_of[15], (D, FD), D ** -0.5, 0.25)
    w_out_down = gaussian(streams_of[16], (FD, C), FD ** -0.5, 0.125)
    return dict(tokens=tokens, date_index=date_index, valid=valid, date_table=date_table, latents=latents, wq_enc=wq_enc, wk_enc=wk_enc, wv_enc=wv_enc, wo_enc=wo_enc, w_lat_up=w_lat_up, w_lat_down=w_lat_down, wq_dec=wq_dec, wk_dec=wk_dec, wv_dec=wv_dec, wo_dec=wo_dec, w_out_up=w_out_up, w_out_down=w_out_down)


def layer_norm(values):
    center = values - lax.optimization_barrier(jnp.mean(values, axis=-1, keepdims=True))
    spread = lax.optimization_barrier(jnp.mean(center * center, axis=-1, keepdims=True))
    return center * lax.rsqrt(spread + 1e-05)

def to_wide(values):
    return lax.optimization_barrier(values.astype(jnp.bfloat16)).astype(jnp.float32)

def reference(tokens, date_index, valid, date_table, latents, wq_enc, wk_enc, wv_enc, wo_enc, w_lat_up, w_lat_down, wq_dec, wk_dec, wv_dec, wo_dec, w_out_up, w_out_down):
    head_size = D // HEADS
    score_scale = head_size ** (-0.5)
    date_shift = jnp.where(date_index[:, None] == 1, date_table[1][None, :], date_table[0][None, :])
    inputs = (tokens.astype(jnp.float32) + date_shift).astype(jnp.bfloat16)
    queries = jnp.dot(latents, wq_enc, preferred_element_type=jnp.float32).astype(jnp.bfloat16)
    queries = queries.reshape(L, HEADS, head_size).transpose(1, 0, 2)
    keys = jnp.dot(inputs, wk_enc, preferred_element_type=jnp.float32).astype(jnp.bfloat16)
    keys = keys.reshape(TOKENS, HEADS, head_size).transpose(1, 0, 2)
    values = jnp.dot(inputs, wv_enc, preferred_element_type=jnp.float32).astype(jnp.bfloat16)
    values = values.reshape(TOKENS, HEADS, head_size).transpose(1, 0, 2)
    usable = valid[None, :] > 0

    def one_head(group):
        head_query, head_key, head_value = group
        scores = jnp.dot(head_query, head_key.T, preferred_element_type=jnp.float32) * score_scale
        scores = jnp.where(usable, scores, -1e+30)
        row_max = lax.optimization_barrier(jnp.max(scores, axis=1, keepdims=True))
        powers = jnp.exp(scores - row_max)
        weight_sum = lax.optimization_barrier(jnp.sum(powers, axis=1, keepdims=True))
        weighted = jnp.dot(powers.astype(jnp.bfloat16), head_value, preferred_element_type=jnp.float32)
        return weighted / weight_sum
    attended = lax.map(one_head, (queries, keys, values))
    attended = attended.transpose(1, 0, 2).reshape(L, D).astype(jnp.bfloat16)
    latent_mid = latents.astype(jnp.float32) + jnp.dot(attended, wo_enc, preferred_element_type=jnp.float32)
    latent_act = jax.nn.gelu(jnp.dot(layer_norm(latent_mid).astype(jnp.bfloat16), w_lat_up, preferred_element_type=jnp.float32)).astype(jnp.bfloat16)
    latent_out = (latent_mid + jnp.dot(latent_act, w_lat_down, preferred_element_type=jnp.float32)).astype(jnp.bfloat16)
    latent_keys = to_wide(jnp.dot(latent_out, wk_dec, preferred_element_type=jnp.float32)).reshape(L, HEADS, head_size)
    latent_values = to_wide(jnp.dot(latent_out, wv_dec, preferred_element_type=jnp.float32)).reshape(L, HEADS, head_size)
    blocks = inputs.reshape(TOKENS // TOK_DEV, TOK_DEV, D)
    flag_blocks = valid.reshape(TOKENS // TOK_DEV, TOK_DEV)

    def decode(group):
        block, flags = group
        token_query = to_wide(jnp.dot(block, wq_dec, preferred_element_type=jnp.float32)).reshape(TOK_DEV, HEADS, head_size)
        scores = jnp.einsum('thd,lhd->thl', token_query, latent_keys) * score_scale
        weights = to_wide(jax.nn.softmax(scores, axis=2))
        mixed = jnp.einsum('thl,lhd->thd', weights, latent_values).reshape(TOK_DEV, D).astype(jnp.bfloat16)
        token_mid = block.astype(jnp.float32) + jnp.dot(mixed, wo_dec, preferred_element_type=jnp.float32)
        token_act = jax.nn.gelu(jnp.dot(layer_norm(token_mid).astype(jnp.bfloat16), w_out_up, preferred_element_type=jnp.float32)).astype(jnp.bfloat16)
        result = jnp.dot(token_act, w_out_down, preferred_element_type=jnp.float32)
        return jnp.where(flags[:, None] > 0, result, jnp.float32(0.0))
    return lax.map(decode, (blocks, flag_blocks)).reshape(TOKENS, C)
```

```python
import functools

import jax
import jax.numpy as jnp
from jax import lax
from jax.experimental import pallas as pl
from jax.experimental.pallas import tpu as pltpu
from jax.sharding import Mesh, PartitionSpec as P

D = 512
HEADS = 8
HEAD = 64
L = 1024
HALF = 512
TOK = 2048
QUARTER = 512
F = 2048
C = 128
SCALE = HEAD ** (-0.5)
NEG = -1e30
PAY = HALF + 8
CHUNK = 40
BF = jnp.bfloat16
F32 = jnp.float32
VMEM_LIMIT = 48 * 1024 * 1024


def mm(a, b):
    return jnp.dot(a, b, preferred_element_type=F32)


def mm_tn(a, b):
    return lax.dot_general(a, b, (((0,), (0,)), ((), ())), preferred_element_type=F32)


def thirds(t):
    high = t.astype(BF)
    rest = t - high.astype(F32)
    mid = rest.astype(BF)
    low = (rest - mid.astype(F32)).astype(BF)
    return high.astype(F32), mid.astype(F32), low.astype(F32)


def date_rows(table):
    zero = jnp.zeros((1, D), F32)
    return jnp.concatenate([*thirds(table[0:1, :]), *thirds(table[1:2, :]), zero, zero], 0)


def flag_rows(date, valid):
    first = jnp.where(date == 1, 0.0, 1.0).astype(F32)
    second = 1.0 - first
    hidden = jnp.where(valid > 0, 0.0, NEG).astype(F32)
    usable = jnp.where(valid > 0, 1.0, 0.0).astype(F32)
    return jnp.concatenate([first] * 3 + [second] * 3 + [hidden, usable], 0)


def row_pick(row, shape):
    return jnp.where(lax.broadcasted_iota(jnp.int32, shape, 0) == row, 1.0, 0.0).astype(F32)


EC = 256
EB = 256


def encode_kernel(
    core, tok, date, valid, table, lat, wq, wk, wv, keep, send, flags, dates, kaug, vt, qaug, sbuf, ot, stat
):
    c = core[0]
    flags[...] = flag_rows(date[...], valid[...])
    dates[...] = date_rows(table[...])
    hide = jnp.concatenate(
        [jnp.where(lax.broadcasted_iota(jnp.int32, (8, 128), 0) == 6, 1.0, 0.0)], 0
    ).astype(F32) * jnp.where(lax.broadcasted_iota(jnp.int32, (8, 128), 1) == 0, 1.0, 0.0)
    for i in range(TOK // EC):
        rows = pl.ds(i * EC, EC)
        marks = flags[:, i * EC : (i + 1) * EC]
        x = (tok[rows, :].astype(F32) + mm_tn(marks, dates[...])).astype(BF)
        kaug[rows, 0:128] = mm(x, wk[...]).astype(BF)
        kaug[rows, 128:256] = mm_tn(marks, hide).astype(BF)
        v = mm(x, wv[...]).astype(BF).astype(F32)
        vt[:, i * EC : (i + 1) * EC] = v.T.astype(BF)
    top = jnp.where(lax.broadcasted_iota(jnp.int32, (128, 1), 0) < HEAD, 1.0, 0.0).astype(F32)
    one = jnp.where(lax.broadcasted_iota(jnp.int32, (128, EB), 0) == 0, 1.0, 0.0).astype(BF)
    for half in range(2):
        start = pl.multiple_of((1 - c if half == 0 else c) * HALF, HALF)
        q = mm(lat[pl.ds(start, HALF), :], wq[...]).astype(BF).astype(F32) * SCALE
        qt = q.T
        for j in range(HALF // EB):
            part = qt[:, j * EB : (j + 1) * EB]
            for h in range(2):
                n = (half * 2 + j) * 2 + h
                mask = top if h == 0 else 1.0 - top
                qaug[n, 0:128, :] = (part * mask).astype(BF)
                qaug[n, 128:256, :] = one

    def block(n, _):
        h = lax.rem(n, 2)
        largest = jnp.full((8, EB), -jnp.inf, F32)
        for i in range(TOK // EC):
            s = mm(kaug[pl.ds(i * EC, EC), :], qaug[n])
            sbuf[pl.ds(i * EC, EC), :] = s
            largest = jnp.maximum(largest, jnp.max(s.reshape(EC // 8, 8, EB), axis=0))
        m = jnp.max(largest, axis=0, keepdims=True)
        total = jnp.zeros((8, EB), F32)
        o = jnp.zeros((HEAD, EB), F32)
        vrow = pl.ds(pl.multiple_of(h * HEAD, HEAD), HEAD)
        for i in range(TOK // EC):
            p = jnp.exp(sbuf[pl.ds(i * EC, EC), :] - m)
            total = total + jnp.sum(p.reshape(EC // 8, 8, EB), axis=0)
            o = o + mm(vt[vrow, i * EC : (i + 1) * EC], p.astype(BF))
        t = jnp.sum(total, axis=0, keepdims=True)
        ot[n] = o / t
        stat[n] = jnp.broadcast_to(m + jnp.log(t), (8, EB))
        return 0

    lax.fori_loop(0, 2 * L // EB, block, 0)
    for half in range(2):
        to = send if half == 0 else keep
        for j in range(HALF // EB):
            n = (half * 2 + j) * 2
            pair = jnp.concatenate([ot[n], ot[n + 1]], 0)
            to[pl.ds(j * EB, EB), :] = pair.T
            for h in range(2):
                for k in range(EB // 128):
                    row = HALF + h * 4 + j * (EB // 128) + k
                    to[row : row + 1, :] = stat[n + h, 0:1, k * 128 : (k + 1) * 128]


def encode(core, tok, date, valid, table, lat, wq, wk, wv):
    blocks = 2 * L // EB
    vm = pl.BlockSpec(memory_space=pltpu.VMEM)
    return pl.pallas_call(
        encode_kernel,
        name="encode",
        out_shape=(jax.ShapeDtypeStruct((PAY, 128), F32),) * 2,
        in_specs=[pl.BlockSpec(memory_space=pltpu.SMEM)] + [vm] * 8,
        out_specs=(vm, vm),
        scratch_shapes=[
            pltpu.VMEM((8, TOK), F32),
            pltpu.VMEM((8, D), F32),
            pltpu.VMEM((TOK, 256), BF),
            pltpu.VMEM((128, TOK), BF),
            pltpu.VMEM((blocks, 256, EB), BF),
            pltpu.VMEM((TOK, EB), F32),
            pltpu.VMEM((blocks, HEAD, EB), F32),
            pltpu.VMEM((blocks, 8, EB), F32),
        ],
        compiler_params=pltpu.CompilerParams(vmem_limit_bytes=VMEM_LIMIT),
        cost_estimate=pl.CostEstimate(
            flops=2 * TOK * D * 256 + 4 * 2 * L * TOK * HEAD + 2 * L * D * 128,
            bytes_accessed=4 << 20,
            transcendentals=2 * L * TOK,
        ),
    )(core, tok, date, valid, table, lat, wq, wk, wv)


def columns(rows):
    return rows.T


def join_pair_kernel(mine, theirs, out):
    a, b = mine[HALF:PAY, :], theirs[HALF:PAY, :]
    top = jnp.maximum(a, b)
    ea, eb = jnp.exp(a - top), jnp.exp(b - top)
    total = ea + eb
    lse = top + jnp.log(total)
    wa, wb = (ea / total).T, (eb / total).T
    left = lax.broadcasted_iota(jnp.int32, (128, 128), 1) < HEAD
    for t in range(4):
        fa = jnp.where(left, wa[:, t : t + 1], wa[:, 4 + t : 5 + t])
        fb = jnp.where(left, wb[:, t : t + 1], wb[:, 4 + t : 5 + t])
        rows = pl.ds(t * 128, 128)
        o = mine[rows, :] * fa + theirs[rows, :] * fb
        for k in range(4):
            out[t * 4 + k, 0:32, :] = o[k * 32 : (k + 1) * 32, :]
            out[t * 4 + k, 32:40, :] = jnp.concatenate(
                [lse[t : t + 1, :], lse[4 + t : 5 + t, :], jnp.zeros((6, 128), F32)], 0
            )


def join_pair(mine, theirs):
    return pl.pallas_call(
        join_pair_kernel,
        name="join_pair",
        out_shape=jax.ShapeDtypeStruct((16, CHUNK, 128), F32),
    )(mine, theirs)


def join_plane_kernel(place, got, out, turned):
    rows = jnp.concatenate([got[s, 32:33, :] for s in range(16)] + [got[s, 33:34, :] for s in range(16)], 0)
    weights = []
    for h in range(2):
        part = rows[h * 16 : (h + 1) * 16, :]
        top = jnp.max(part, axis=0, keepdims=True)
        e = jnp.exp(part - top)
        weights.append(e / jnp.sum(e, axis=0, keepdims=True))
    turned[:, 0:32] = jnp.concatenate(weights, 0).T
    start = pl.multiple_of(lax.rem(place[0], 4) * 32, 32)
    cols = turned[pl.ds(start, 32), :]
    left = lax.broadcasted_iota(jnp.int32, (32, 128), 1) < HEAD
    o = jnp.zeros((32, 128), F32)
    for s in range(16):
        o = o + got[s, 0:32, :] * jnp.where(left, cols[:, s : s + 1], cols[:, 16 + s : 17 + s])
    out[...] = jnp.broadcast_to(o.astype(BF)[None], (64, 32, 128))


def join_plane(place, got):
    return pl.pallas_call(
        join_plane_kernel,
        name="join_plane",
        out_shape=jax.ShapeDtypeStruct((64, 32, 128), BF),
        in_specs=[pl.BlockSpec(memory_space=pltpu.SMEM), pl.BlockSpec(memory_space=pltpu.VMEM)],
        out_specs=pl.BlockSpec(memory_space=pltpu.VMEM),
        scratch_shapes=[pltpu.VMEM((128, 128), F32)],
    )(place, got)


def norm(v):
    center = v - jnp.mean(v, axis=-1, keepdims=True)
    spread = jnp.mean(center * center, axis=-1, keepdims=True)
    return center * lax.rsqrt(spread + 1e-05)


def latent_kernel(core, att, lat, wo, wup, wdown, out):
    start = pl.multiple_of(core[0] * HALF, HALF)
    for i in range(HALF // 128):
        rows = pl.ds(i * 128, 128)
        a = jnp.concatenate([att[x, rows, :] for x in range(4)], 1)
        mid = lat[pl.ds(start + i * 128, 128), :].astype(F32) + mm(a, wo[...])
        act = jax.nn.gelu(mm(norm(mid).astype(BF), wup[...])).astype(BF)
        out[rows, :] = (mid + mm(act, wdown[...])).astype(BF)


def latent(core, att, lat, wo, wup, wdown):
    vm = pl.BlockSpec(memory_space=pltpu.VMEM)
    return pl.pallas_call(
        latent_kernel,
        name="latent",
        out_shape=jax.ShapeDtypeStruct((HALF, D), BF),
        in_specs=[pl.BlockSpec(memory_space=pltpu.SMEM)] + [vm] * 5,
        out_specs=vm,
        compiler_params=pltpu.CompilerParams(vmem_limit_bytes=VMEM_LIMIT),
    )(core, att, lat, wo, wup, wdown)


def decode_kernel(
    quarter, tok, date, valid, table, la, lb, wq, wk, wv, wo, wup, wdown, out, kbuf, vt, qt, sbuf, dt
):
    start = pl.multiple_of(quarter[0] * QUARTER, QUARTER)
    marks = flag_rows(date[:, pl.ds(start, QUARTER)], valid[:, pl.ds(start, QUARTER)])
    x = (tok[pl.ds(start, QUARTER), :].astype(F32) + mm_tn(marks, date_rows(table[...]))).astype(BF)
    qt[...] = (mm(x, wq[...]).astype(BF).astype(F32) * SCALE).T.astype(BF)
    for g, ref in enumerate((la, lb)):
        rows = pl.ds(g * HALF, HALF)
        kbuf[rows, :] = mm(ref[...], wk[...]).astype(BF)
        vt[:, g * HALF : (g + 1) * HALF] = mm(ref[...], wv[...]).astype(BF).astype(F32).T.astype(BF)
    zero = jnp.zeros((HEAD, QUARTER), BF)
    for h in range(HEADS):
        pair = h // 2 * 128
        own = qt[h * HEAD : (h + 1) * HEAD, :]
        q = jnp.concatenate([own, zero] if h % 2 == 0 else [zero, own], 0)
        largest = jnp.full((8, QUARTER), -jnp.inf, F32)
        for i in range(L // 256):
            s = mm(kbuf[pl.ds(i * 256, 256), pair : pair + 128], q)
            sbuf[h % 2, pl.ds(i * 256, 256), :] = s
            largest = jnp.maximum(largest, jnp.max(s.reshape(32, 8, QUARTER), axis=0))
        m = jnp.max(largest, axis=0, keepdims=True)
        total = jnp.zeros((8, QUARTER), F32)
        for i in range(L // 256):
            p = jnp.exp(sbuf[h % 2, pl.ds(i * 256, 256), :] - m)
            sbuf[h % 2, pl.ds(i * 256, 256), :] = p
            total = total + jnp.sum(p.reshape(32, 8, QUARTER), axis=0)
        inverse = 1.0 / jnp.sum(total, axis=0, keepdims=True)
        o = jnp.zeros((HEAD, QUARTER), F32)
        for i in range(L // 256):
            p = (sbuf[h % 2, pl.ds(i * 256, 256), :] * inverse).astype(BF)
            o = o + mm(vt[h * HEAD : (h + 1) * HEAD, i * 256 : (i + 1) * 256], p)
        dt[h * HEAD : (h + 1) * HEAD, :] = o
    usable = row_pick(7, (8, C))
    for i in range(QUARTER // 128):
        decoded = dt[:, i * 128 : (i + 1) * 128].T.astype(BF)
        own = x[i * 128 : (i + 1) * 128, :]
        mid = own.astype(F32) + mm(decoded, wo[...])
        act = jax.nn.gelu(mm(norm(mid).astype(BF), wup[...])).astype(BF)
        keep = mm_tn(marks[:, i * 128 : (i + 1) * 128], usable)
        out[pl.ds(i * 128, 128), :] = jnp.where(keep > 0.5, mm(act, wdown[...]), 0.0)


def decode(quarter, tok, date, valid, table, la, lb, wq, wk, wv, wo, wup, wdown):
    vm = pl.BlockSpec(memory_space=pltpu.VMEM)
    return pl.pallas_call(
        decode_kernel,
        name="decode",
        out_shape=jax.ShapeDtypeStruct((QUARTER, C), F32),
        in_specs=[pl.BlockSpec(memory_space=pltpu.SMEM)] + [vm] * 12,
        out_specs=vm,
        scratch_shapes=[
            pltpu.VMEM((L, D), BF),
            pltpu.VMEM((D, L), BF),
            pltpu.VMEM((D, QUARTER), BF),
            pltpu.VMEM((2, L, QUARTER), F32),
            pltpu.VMEM((D, QUARTER), F32),
        ],
        compiler_params=pltpu.CompilerParams(vmem_limit_bytes=VMEM_LIMIT),
    )(quarter, tok, date, valid, table, la, lb, wq, wk, wv, wo, wup, wdown)


def per_device(
    tokens,
    date_index,
    valid,
    date_table,
    latents,
    wq_enc,
    wk_enc,
    wv_enc,
    wo_enc,
    w_lat_up,
    w_lat_down,
    wq_dec,
    wk_dec,
    wv_dec,
    wo_dec,
    w_out_up,
    w_out_down,
):
    core = lax.axis_index("c").astype(jnp.int32).reshape(1)
    place = lax.axis_index(("y", "z")).astype(jnp.int32).reshape(1)
    quarter = lax.axis_index("x").astype(jnp.int32).reshape(1)
    date = date_index.reshape(1, TOK)
    flag = valid.reshape(1, TOK)
    swap = [(0, 1), (1, 0)]
    keep, send = encode(core, tokens, date, flag, date_table, latents, wq_enc, wk_enc, wv_enc)
    other = lax.ppermute(send, "c", swap)
    chunks = join_pair(keep, other)
    got = lax.all_to_all(chunks, ("y", "z"), 0, 0)
    copies = join_plane(place, got)
    attended = lax.all_to_all(copies, ("x", "y", "z"), 0, 0).reshape(4, HALF, 128)
    own = latent(core, attended, latents, wo_enc, w_lat_up, w_lat_down)
    others = lax.ppermute(own, "c", swap)
    return decode(
        quarter, tokens, date, flag, date_table, own, others,
        wq_dec, wk_dec, wv_dec, wo_dec, w_out_up, w_out_down,
    )


def solution(mesh):
    parts = Mesh(mesh.devices.reshape(4, 4, 4, 2), ("x", "y", "z", "c"))
    tok = ("y", "z", "c")
    in_specs = (
        P(tok, None),
        P(tok),
        P(tok),
        P(),
        P(),
        P(None, "x"),
        P(None, "x"),
        P(None, "x"),
        P(),
        P(),
        P(),
        P(),
        P(),
        P(),
        P(),
        P(),
        P(),
    )
    out_specs = P((*tok, "x"), None)
    return jax.shard_map(
        per_device, mesh=parts, in_specs=in_specs, out_specs=out_specs, check_vma=False
    )
```

```python
import functools

import jax
import jax.numpy as jnp
from jax import lax
from jax.experimental import pallas as pl
from jax.experimental.pallas import tpu as pltpu
from jax.sharding import Mesh, PartitionSpec as P

D = 512
HEADS = 8
HEAD = 64
L = 1024
HALF = 512
TOK = 2048
QUARTER = 512
F = 2048
C = 128
SCALE = HEAD ** (-0.5)
LOG2E = 1.4426950408889634
NEG = -1e30
PAY = HALF + 8
CHUNK = 40
BF = jnp.bfloat16
F32 = jnp.float32
VMEM_LIMIT = 20 * 1024 * 1024
JOIN_LIMIT = 8 * 1024 * 1024


def mm(a, b):
    return jnp.dot(a, b, preferred_element_type=F32)


def mm_tn(a, b):
    return lax.dot_general(a, b, (((0,), (0,)), ((), ())), preferred_element_type=F32)


def thirds(t):
    high = t.astype(BF)
    rest = t - high.astype(F32)
    mid = rest.astype(BF)
    low = (rest - mid.astype(F32)).astype(BF)
    return high.astype(F32), mid.astype(F32), low.astype(F32)


def date_rows(table):
    zero = jnp.zeros((1, D), F32)
    return jnp.concatenate([*thirds(table[0:1, :]), *thirds(table[1:2, :]), zero, zero], 0)


def flag_rows(date, valid):
    first = jnp.where(date == 1, 0.0, 1.0).astype(F32)
    second = 1.0 - first
    hidden = jnp.where(valid > 0, 0.0, NEG).astype(F32)
    usable = jnp.where(valid > 0, 1.0, 0.0).astype(F32)
    return jnp.concatenate([first] * 3 + [second] * 3 + [hidden, usable], 0)


def row_pick(row, shape):
    return jnp.where(lax.broadcasted_iota(jnp.int32, shape, 0) == row, 1.0, 0.0).astype(F32)


EC = 256
EB = 256
EP = 4
ONES = 16


def fetch(pairs, sems):
    copies = [pltpu.make_async_copy(a, b, sems.at[i]) for i, (a, b) in enumerate(pairs)]
    for copy in copies:
        copy.start()
    return copies


def split_query(q):
    scaled = q.astype(F32) * (SCALE * LOG2E)
    high = scaled.astype(BF)
    return high, (scaled - high.astype(F32)).astype(BF)


def pair_query(high, low, odd):
    zero = jnp.zeros(high.shape, BF)
    rows = [zero, high, zero, low] if odd else [high, zero, low, zero]
    return jnp.concatenate(rows, 0)


def score_step(keys, query, to, rows, largest):
    s = mm(jnp.concatenate([keys, keys], 1), query)
    to[rows, :] = s
    return jnp.maximum(largest, jnp.max(s.reshape(s.shape[0] // 8, 8, s.shape[1]), axis=0))


def weight_step(values, frm, rows, m):
    return mm(values, jnp.exp2(frm[rows, :] - m).astype(BF))


def encode_kernel(
    where, tok_h, date_h, valid_h, table_h, lat_h, wq_h, wk_h, wv_h, keep, send,
    tok, date, valid, table, lat, wq, wk, wv, flags, dates, kbuf, vt, qbuf, s0, s1, ot, stat, sems,
):
    c = where[0]
    part = TOK // EP
    pairs = [(wq_h, wq), (lat_h, lat), (date_h, date), (valid_h, valid), (table_h, table), (wk_h, wk), (wv_h, wv)]
    pairs += [(tok_h.at[pl.ds(i * part, part)], tok.at[pl.ds(i * part, part)]) for i in range(EP)]
    copies = fetch(pairs, sems)
    copies[0].wait()
    copies[1].wait()
    for half in range(2):
        start = pl.multiple_of((1 - c if half == 0 else c) * HALF, HALF)
        q = mm(lat[pl.ds(start, HALF), :], wq[...]).astype(BF).astype(F32)
        qt = q.T.astype(BF)
        for j in range(HALF // EB):
            high, low = split_query(qt[:, j * EB : (j + 1) * EB])
            for h in range(2):
                own = slice(h * HEAD, (h + 1) * HEAD)
                qbuf[(half * 2 + j) * 2 + h] = pair_query(high[own], low[own], h == 1)
    for copy in copies[2:7]:
        copy.wait()
    flags[...] = flag_rows(date[...], valid[...])
    dates[...] = date_rows(table[...])
    usable = row_pick(7, (8, 128))
    for h in range(2):
        vt[h, HEAD : HEAD + ONES, :] = jnp.concatenate(
            [flags[7:8, :], jnp.zeros((ONES - 1, TOK), F32)], 0
        ).astype(BF)
    for i in range(TOK // EC):
        if i % (TOK // EC // EP) == 0:
            copies[7 + i // (TOK // EC // EP)].wait()
        rows = pl.ds(i * EC, EC)
        cols = slice(i * EC, (i + 1) * EC)
        marks = flags[:, cols]
        x = (tok[rows, :].astype(F32) + mm_tn(marks, dates[...])).astype(BF)
        k = mm(x, wk[...])
        first = jnp.broadcast_to(k.reshape(EC // 16, 16, 128)[:, 0:1, :], (EC // 16, 16, 128)).reshape(EC, 128)
        kbuf[rows, :] = jnp.where(mm_tn(marks, usable) > 0.5, k, first).astype(BF)
        v = (mm(x, wv[...]).astype(BF).astype(F32).T * flags[7:8, cols]).astype(BF)
        vt[0, 0:HEAD, cols] = v[0:HEAD]
        vt[1, 0:HEAD, cols] = v[HEAD:128]

    low_start = jnp.full((8, EB), -jnp.inf, F32)
    chunks = TOK // EC
    blocks = 2 * L // EB

    def scores(n, to):
        largest = low_start
        for i in range(chunks):
            largest = score_step(kbuf[pl.ds(i * EC, EC), :], qbuf[n], to, pl.ds(i * EC, EC), largest)
        return jnp.max(largest, axis=0, keepdims=True)

    def finish(n, o, m):
        t = o[HEAD : HEAD + 1, :]
        ot[n] = o[0:HEAD, :] / t
        stat[n] = jnp.broadcast_to(m + jnp.log2(t), (8, EB))

    def both(n, frm, to, m, odd):
        largest = low_start
        o = jnp.zeros((HEAD + ONES, EB), F32)
        for i in range(chunks):
            rows = pl.ds(i * EC, EC)
            largest = score_step(kbuf[rows, :], qbuf[n + 1], to, rows, largest)
            o = o + weight_step(vt[odd, :, i * EC : (i + 1) * EC], frm, rows, m)
        finish(n, o, m)
        return jnp.max(largest, axis=0, keepdims=True)

    def two(g, m):
        n = g * 2
        m = both(n, s0, s1, m, 0)
        return both(n + 1, s1, s0, m, 1)

    m = scores(0, s0)
    m = lax.fori_loop(0, blocks // 2 - 1, two, m)
    m = both(blocks - 2, s0, s1, m, 0)
    o = jnp.zeros((HEAD + ONES, EB), F32)
    for i in range(chunks):
        o = o + weight_step(vt[1, :, i * EC : (i + 1) * EC], s1, pl.ds(i * EC, EC), m)
    finish(blocks - 1, o, m)
    for half in range(2):
        to = send if half == 0 else keep
        for j in range(HALF // EB):
            n = (half * 2 + j) * 2
            pair = jnp.concatenate([ot[n], ot[n + 1]], 0)
            to[pl.ds(j * EB, EB), :] = pair.T
            for h in range(2):
                for k in range(EB // 128):
                    row = HALF + h * 4 + j * (EB // 128) + k
                    to[row : row + 1, :] = stat[n + h, 0:1, k * 128 : (k + 1) * 128]


def encode(where, tok, date, valid, table, lat, wq, wk, wv):
    blocks = 2 * L // EB
    vm = pl.BlockSpec(memory_space=pltpu.VMEM)
    hbm = pl.BlockSpec(memory_space=pltpu.HBM)
    return pl.pallas_call(
        encode_kernel,
        name="encode",
        out_shape=(jax.ShapeDtypeStruct((PAY, 128), F32),) * 2,
        in_specs=[pl.BlockSpec(memory_space=pltpu.SMEM)] + [hbm] * 8,
        out_specs=(vm, vm),
        scratch_shapes=[
            pltpu.VMEM((TOK, D), BF),
            pltpu.VMEM((1, TOK), jnp.int32),
            pltpu.VMEM((1, TOK), jnp.int32),
            pltpu.VMEM((2, D), F32),
            pltpu.VMEM((L, D), BF),
            pltpu.VMEM((D, 128), BF),
            pltpu.VMEM((D, 128), BF),
            pltpu.VMEM((D, 128), BF),
            pltpu.VMEM((8, TOK), F32),
            pltpu.VMEM((8, D), F32),
            pltpu.VMEM((TOK, 128), BF),
            pltpu.VMEM((2, HEAD + ONES, TOK), BF),
            pltpu.VMEM((blocks, 256, EB), BF),
            pltpu.VMEM((TOK, EB), F32),
            pltpu.VMEM((TOK, EB), F32),
            pltpu.VMEM((blocks, HEAD, EB), F32),
            pltpu.VMEM((blocks, 8, EB), F32),
            pltpu.SemaphoreType.DMA((7 + EP,)),
        ],
        compiler_params=pltpu.CompilerParams(vmem_limit_bytes=VMEM_LIMIT),
        cost_estimate=pl.CostEstimate(
            flops=2 * TOK * D * 256 + 4 * 2 * L * TOK * HEAD + 2 * L * D * 128,
            bytes_accessed=4 << 20,
            transcendentals=2 * L * TOK,
        ),
    )(where, *[pltpu.with_memory_space_constraint(a, pltpu.HBM) for a in (tok, date, valid, table, lat, wq, wk, wv)])


def join_pair_kernel(mine, theirs, out):
    a, b = mine[HALF:PAY, :], theirs[HALF:PAY, :]
    top = jnp.maximum(a, b)
    ea, eb = jnp.exp2(a - top), jnp.exp2(b - top)
    total = ea + eb
    lse = top + jnp.log2(total)
    wa, wb = (ea / total).T, (eb / total).T
    left = lax.broadcasted_iota(jnp.int32, (128, 128), 1) < HEAD
    for t in range(4):
        fa = jnp.where(left, wa[:, t : t + 1], wa[:, 4 + t : 5 + t])
        fb = jnp.where(left, wb[:, t : t + 1], wb[:, 4 + t : 5 + t])
        rows = pl.ds(t * 128, 128)
        o = mine[rows, :] * fa + theirs[rows, :] * fb
        for k in range(4):
            out[t * 4 + k, 0:32, :] = o[k * 32 : (k + 1) * 32, :]
            out[t * 4 + k, 32:40, :] = jnp.concatenate(
                [lse[t : t + 1, :], lse[4 + t : 5 + t, :], jnp.zeros((6, 128), F32)], 0
            )


def join_pair(mine, theirs):
    return pl.pallas_call(
        join_pair_kernel,
        name="join_pair",
        out_shape=jax.ShapeDtypeStruct((16, CHUNK, 128), F32),
        in_specs=[pl.BlockSpec(memory_space=pltpu.VMEM)] * 2,
        out_specs=pl.BlockSpec(memory_space=pltpu.VMEM),
        compiler_params=pltpu.CompilerParams(vmem_limit_bytes=JOIN_LIMIT),
    )(mine, theirs)


def join_plane_kernel(where, got, out, turned):
    rows = jnp.concatenate([got[s, 32:33, :] for s in range(16)] + [got[s, 33:34, :] for s in range(16)], 0)
    weights = []
    for h in range(2):
        part = rows[h * 16 : (h + 1) * 16, :]
        top = jnp.max(part, axis=0, keepdims=True)
        e = jnp.exp2(part - top)
        weights.append(e / jnp.sum(e, axis=0, keepdims=True))
    turned[:, 0:32] = jnp.concatenate(weights, 0).T
    start = pl.multiple_of(lax.rem(where[1], 4) * 32, 32)
    cols = turned[pl.ds(start, 32), :]
    left = lax.broadcasted_iota(jnp.int32, (32, 128), 1) < HEAD
    o = jnp.zeros((32, 128), F32)
    for s in range(16):
        o = o + got[s, 0:32, :] * jnp.where(left, cols[:, s : s + 1], cols[:, 16 + s : 17 + s])
    out[...] = jnp.broadcast_to(o.astype(BF)[None], (64, 32, 128))


def join_plane(where, got):
    return pl.pallas_call(
        join_plane_kernel,
        name="join_plane",
        out_shape=jax.ShapeDtypeStruct((64, 32, 128), BF),
        in_specs=[pl.BlockSpec(memory_space=pltpu.SMEM), pl.BlockSpec(memory_space=pltpu.VMEM)],
        out_specs=pl.BlockSpec(memory_space=pltpu.VMEM),
        scratch_shapes=[pltpu.VMEM((128, 128), F32)],
        compiler_params=pltpu.CompilerParams(vmem_limit_bytes=JOIN_LIMIT),
    )(where, got)


FB = 512


def norm(v):
    center = v - jnp.mean(v, axis=-1, keepdims=True)
    spread = jnp.mean(center * center, axis=-1, keepdims=True)
    return center * lax.rsqrt(spread + 1e-05)


def latent_kernel(where, att, lat, wo, wup, wdown, out):
    start = pl.multiple_of(where[0] * HALF, HALF)
    a = jnp.concatenate([att[x] for x in range(4)], 1)
    mid = lat[pl.ds(start, HALF), :].astype(F32) + mm(a, wo[...])
    ready = norm(mid).astype(BF)
    for i in range(F // FB):
        act = jax.nn.gelu(mm(ready, wup[:, i * FB : (i + 1) * FB])).astype(BF)
        mid = mid + mm(act, wdown[i * FB : (i + 1) * FB, :])
    out[...] = mid.astype(BF)


def latent(where, att, lat, wo, wup, wdown):
    vm = pl.BlockSpec(memory_space=pltpu.VMEM)
    return pl.pallas_call(
        latent_kernel,
        name="latent",
        out_shape=jax.ShapeDtypeStruct((HALF, D), BF),
        in_specs=[pl.BlockSpec(memory_space=pltpu.SMEM)] + [vm] * 5,
        out_specs=vm,
        compiler_params=pltpu.CompilerParams(vmem_limit_bytes=VMEM_LIMIT),
    )(where, att, lat, wo, wup, wdown)


DC = 256


def decode_kernel(
    where, tok, date, valid, table, la, lb, wq, wk, wv, wo, wup, wdown, out, kbuf, vt, qt, s0, s1, dt
):
    start = pl.multiple_of(where[2] * QUARTER, QUARTER)
    cut = pl.ds(start, QUARTER)
    marks = flag_rows(date[:, cut], valid[:, cut])
    x = (tok[cut, :].astype(F32) + mm_tn(marks, date_rows(table[...]))).astype(BF)
    qt[...] = mm(x, wq[...]).astype(BF).astype(F32).T.astype(BF)
    for g, ref in enumerate((la, lb)):
        rows = pl.ds(g * HALF, HALF)
        kbuf[rows, :] = mm(ref[...], wk[...]).astype(BF)
        v = mm(ref[...], wv[...]).astype(BF).astype(F32).T.astype(BF)
        for h in range(HEADS):
            vt[h, 0:HEAD, g * HALF : (g + 1) * HALF] = v[h * HEAD : (h + 1) * HEAD, :]
            vt[h, HEAD : HEAD + ONES, g * HALF : (g + 1) * HALF] = row_pick(0, (ONES, HALF)).astype(BF)
    low_start = jnp.full((8, QUARTER), -jnp.inf, F32)
    m = None
    for h in range(HEADS + 1):
        to, frm = (s0, s1) if h % 2 == 0 else (s1, s0)
        largest = low_start
        o = jnp.zeros((HEAD + ONES, QUARTER), F32)
        if h < HEADS:
            high, low = split_query(qt[h * HEAD : (h + 1) * HEAD, :])
            query = pair_query(high, low, h % 2 == 1)
            pair = h // 2 * 128
        for i in range(L // DC):
            rows = pl.ds(i * DC, DC)
            if h < HEADS:
                largest = score_step(kbuf[rows, pair : pair + 128], query, to, rows, largest)
            if h > 0:
                o = o + weight_step(vt[h - 1, :, i * DC : (i + 1) * DC], frm, rows, m)
        if h > 0:
            dt[(h - 1) * HEAD : h * HEAD, :] = o[0:HEAD, :] / o[HEAD : HEAD + 1, :]
        if h < HEADS:
            m = jnp.max(largest, axis=0, keepdims=True)
    decoded = dt[...].T.astype(BF)
    mid = x.astype(F32) + mm(decoded, wo[...])
    ready = norm(mid).astype(BF)
    result = jnp.zeros((QUARTER, C), F32)
    for i in range(F // FB):
        act = jax.nn.gelu(mm(ready, wup[:, i * FB : (i + 1) * FB])).astype(BF)
        result = result + mm(act, wdown[i * FB : (i + 1) * FB, :])
    out[...] = jnp.where(mm_tn(marks, row_pick(7, (8, C))) > 0.5, result, 0.0)


def decode(where, tok, date, valid, table, la, lb, wq, wk, wv, wo, wup, wdown):
    vm = pl.BlockSpec(memory_space=pltpu.VMEM)
    return pl.pallas_call(
        decode_kernel,
        name="decode",
        out_shape=jax.ShapeDtypeStruct((QUARTER, C), F32),
        in_specs=[pl.BlockSpec(memory_space=pltpu.SMEM)] + [vm] * 12,
        out_specs=vm,
        scratch_shapes=[
            pltpu.VMEM((L, D), BF),
            pltpu.VMEM((HEADS, HEAD + ONES, L), BF),
            pltpu.VMEM((D, QUARTER), BF),
            pltpu.VMEM((L, QUARTER), F32),
            pltpu.VMEM((L, QUARTER), F32),
            pltpu.VMEM((D, QUARTER), F32),
        ],
        compiler_params=pltpu.CompilerParams(vmem_limit_bytes=VMEM_LIMIT),
    )(where, tok, date, valid, table, la, lb, wq, wk, wv, wo, wup, wdown)


def per_device(
    tokens,
    date_index,
    valid,
    date_table,
    latents,
    wq_enc,
    wk_enc,
    wv_enc,
    wo_enc,
    w_lat_up,
    w_lat_down,
    wq_dec,
    wk_dec,
    wv_dec,
    wo_dec,
    w_out_up,
    w_out_down,
):
    places = [lax.axis_index("c"), lax.axis_index(("y", "z")), lax.axis_index("x")]
    where = jnp.stack(places).astype(jnp.int32)
    date = date_index.reshape(1, TOK)
    flag = valid.reshape(1, TOK)
    swap = [(0, 1), (1, 0)]
    keep, send = encode(where, tokens, date, flag, date_table, latents, wq_enc, wk_enc, wv_enc)
    other = lax.ppermute(send, "c", swap)
    chunks = join_pair(keep, other)
    got = lax.all_to_all(chunks, ("y", "z"), 0, 0)
    copies = join_plane(where, got)
    attended = lax.all_to_all(copies, ("x", "y", "z"), 0, 0).reshape(4, HALF, 128)
    own = latent(where, attended, latents, wo_enc, w_lat_up, w_lat_down)
    others = lax.ppermute(own, "c", swap)
    return decode(
        where, tokens, date, flag, date_table, own, others,
        wq_dec, wk_dec, wv_dec, wo_dec, w_out_up, w_out_down,
    )


def solution(mesh):
    parts = Mesh(mesh.devices.reshape(4, 4, 4, 2), ("x", "y", "z", "c"))
    tok = ("y", "z", "c")
    in_specs = (
        P(tok, None),
        P(tok),
        P(tok),
        P(),
        P(),
        P(None, "x"),
        P(None, "x"),
        P(None, "x"),
        P(),
        P(),
        P(),
        P(),
        P(),
        P(),
        P(),
        P(),
        P(),
    )
    out_specs = P((*tok, "x"), None)
    return jax.shard_map(
        per_device, mesh=parts, in_specs=in_specs, out_specs=out_specs, check_vma=False
    )
```

```python
import functools

import jax
import jax.numpy as jnp
from jax import lax
from jax.experimental import pallas as pl
from jax.experimental.pallas import tpu as pltpu
from jax.sharding import Mesh, PartitionSpec as P

D = 512
HEADS = 8
HEAD = 64
L = 1024
HALF = 512
TOK = 2048
QUARTER = 512
F = 2048
C = 128
SCALE = HEAD ** (-0.5)
LOG2E = 1.4426950408889634
NEG = -1e30
PAY = HALF + 8
CHUNK = 40
BF = jnp.bfloat16
F32 = jnp.float32
VMEM_LIMIT = 20 * 1024 * 1024
JOIN_LIMIT = 8 * 1024 * 1024


def mm(a, b):
    return jnp.dot(a, b, preferred_element_type=F32)


def row_pick(row, shape):
    return jnp.where(lax.broadcasted_iota(jnp.int32, shape, 0) == row, 1.0, 0.0).astype(F32)


EC = 256
EB = 256
ES = 512
ONES = 16


def fetch(pairs, sems):
    copies = [pltpu.make_async_copy(a, b, sems.at[i]) for i, (a, b) in enumerate(pairs)]
    for copy in copies:
        copy.start()
    return copies


def split_query(q):
    scaled = q.astype(F32) * (SCALE * LOG2E)
    high = scaled.astype(BF)
    return high, (scaled - high.astype(F32)).astype(BF)


def pair_query(high, low, odd):
    zero = jnp.zeros(high.shape, BF)
    rows = [zero, high, zero, low] if odd else [high, zero, low, zero]
    return jnp.concatenate(rows, 0)


def score_step(keys, query, to, rows, largest):
    s = mm(jnp.concatenate([keys, keys], 1), query)
    to[rows, :] = s
    return jnp.maximum(largest, jnp.max(s.reshape(s.shape[0] // 8, 8, s.shape[1]), axis=0))


def weight_step(values, frm, rows, m):
    return mm(values, jnp.exp2(frm[rows, :] - m).astype(BF))


def encode_kernel(
    tok_h, date_h, valid_h, table_h, lat_h, wq_h, wk_h, wv_h, keep, send,
    tok, date, valid, table, lat, wq, wkv, kbuf, vt, qbuf, s0, s1, sems,
):
    c = lax.axis_index("c")
    pairs = [(wq_h, wq), (lat_h, lat), (date_h, date), (valid_h, valid), (table_h, table)]
    pairs += [(wk_h, wkv.at[:, 0:128]), (wv_h, wkv.at[:, 128:256]), (tok_h, tok)]
    copies = fetch(pairs, sems)
    copies[0].wait()
    copies[1].wait()
    for half in range(2):
        start = pl.multiple_of((1 - c if half == 0 else c) * HALF, HALF)
        q = mm(lat[pl.ds(start, HALF), :], wq[...]).astype(BF).astype(F32)
        qt = q.T.astype(BF)
        for j in range(HALF // EB):
            high, low = split_query(qt[:, j * EB : (j + 1) * EB])
            for h in range(2):
                own = slice(h * HEAD, (h + 1) * HEAD)
                qbuf[(half * 2 + j) * 2 + h] = pair_query(high[own], low[own], h == 1)
    for copy in copies[2:]:
        copy.wait()
    usable = jnp.where(valid[...] > 0, 1.0, 0.0).astype(F32)
    second = jnp.where(date[...] == 1, 1.0, 0.0).astype(F32)
    flags = jnp.concatenate([second, usable, jnp.zeros((6, TOK), F32)], 0)
    row0, row1 = table[0:1, :], table[1:2, :]
    for h in range(2):
        vt[h, HEAD : HEAD + ONES, :] = jnp.concatenate([usable, jnp.zeros((ONES - 1, TOK), F32)], 0).astype(BF)
    for i in range(TOK // EC):
        rows = pl.ds(i * EC, EC)
        cols = slice(i * EC, (i + 1) * EC)
        marks = flags[:, cols].T
        shift = jnp.where(jnp.broadcast_to(marks[:, 0:1], (EC, D)) > 0.5, row1, row0)
        x = (tok[rows, :].astype(F32) + shift).astype(BF)
        kv = mm(x, wkv[...])
        k = kv[:, 0:128]
        first = jnp.broadcast_to(k.reshape(EC // 16, 16, 128)[:, 0:1, :], (EC // 16, 16, 128)).reshape(EC, 128)
        kbuf[rows, :] = jnp.where(jnp.broadcast_to(marks[:, 1:2], (EC, 128)) > 0.5, k, first).astype(BF)
        v = (kv[:, 128:256].astype(BF).astype(F32).T * usable[:, cols]).astype(BF)
        vt[0, 0:HEAD, cols] = v[0:HEAD]
        vt[1, 0:HEAD, cols] = v[HEAD:128]

    low_start = jnp.full((8, EB), -jnp.inf, F32)
    blocks = 2 * L // EB

    def step(n, frm, to, m, odd, score, weigh):
        largest = low_start
        o = jnp.zeros((HEAD + ONES, EB), F32)
        for i in range(TOK // ES):
            rows = pl.ds(i * ES, ES)
            if score:
                largest = score_step(kbuf[rows, :], qbuf[n + 1], to, rows, largest)
            if weigh:
                o = o + weight_step(vt[odd, :, i * ES : (i + 1) * ES], frm, rows, m)
        t = o[HEAD : HEAD + 1, :]
        return jnp.max(largest, axis=0, keepdims=True), o[0:HEAD, :] / t if weigh else None, m + jnp.log2(t)

    def put(to, j, o0, o1, l0, l1):
        to[pl.ds(pl.multiple_of(j * EB, EB), EB), :] = jnp.concatenate([o0, o1], 0).T
        for h, line in enumerate((l0, l1)):
            for k in range(EB // 128):
                to[pl.ds(HALF + h * 4 + j * (EB // 128) + k, 1), :] = line[:, k * 128 : (k + 1) * 128]

    m, _, _ = step(-1, s1, s0, jnp.zeros((1, EB), F32), 0, True, False)
    for j in range(L // EB):
        to = send if j < HALF // EB else keep
        m, o0, l0 = step(2 * j, s0, s1, m, 0, True, True)
        m, o1, l1 = step(2 * j + 1, s1, s0, m, 1, j < L // EB - 1, True)
        put(to, j % (HALF // EB), o0, o1, l0, l1)


def encode(tok, date, valid, table, lat, wq, wk, wv):
    blocks = 2 * L // EB
    vm = pl.BlockSpec(memory_space=pltpu.VMEM)
    hbm = pl.BlockSpec(memory_space=pltpu.HBM)
    return pl.pallas_call(
        encode_kernel,
        name="encode",
        out_shape=(jax.ShapeDtypeStruct((PAY, 128), F32),) * 2,
        in_specs=[hbm] * 8,
        out_specs=(vm, vm),
        scratch_shapes=[
            pltpu.VMEM((TOK, D), BF),
            pltpu.VMEM((1, TOK), jnp.int32),
            pltpu.VMEM((1, TOK), jnp.int32),
            pltpu.VMEM((2, D), F32),
            pltpu.VMEM((L, D), BF),
            pltpu.VMEM((D, 128), BF),
            pltpu.VMEM((D, 256), BF),
            pltpu.VMEM((TOK, 128), BF),
            pltpu.VMEM((2, HEAD + ONES, TOK), BF),
            pltpu.VMEM((blocks, 256, EB), BF),
            pltpu.VMEM((TOK, EB), F32),
            pltpu.VMEM((TOK, EB), F32),
            pltpu.SemaphoreType.DMA((8,)),
        ],
        compiler_params=pltpu.CompilerParams(vmem_limit_bytes=VMEM_LIMIT),
        cost_estimate=pl.CostEstimate(
            flops=2 * TOK * D * 256 + 4 * 2 * L * TOK * HEAD + 2 * L * D * 128,
            bytes_accessed=4 << 20,
            transcendentals=2 * L * TOK,
        ),
    )(*[pltpu.with_memory_space_constraint(a, pltpu.HBM) for a in (tok, date, valid, table, lat, wq, wk, wv)])


def join_pair_kernel(mine, theirs, out):
    a, b = mine[HALF:PAY, :], theirs[HALF:PAY, :]
    top = jnp.maximum(a, b)
    ea, eb = jnp.exp2(a - top), jnp.exp2(b - top)
    total = ea + eb
    lse = top + jnp.log2(total)
    wa, wb = (ea / total).T, (eb / total).T
    left = lax.broadcasted_iota(jnp.int32, (128, 128), 1) < HEAD
    for t in range(4):
        fa = jnp.where(left, wa[:, t : t + 1], wa[:, 4 + t : 5 + t])
        fb = jnp.where(left, wb[:, t : t + 1], wb[:, 4 + t : 5 + t])
        rows = pl.ds(t * 128, 128)
        o = mine[rows, :] * fa + theirs[rows, :] * fb
        for k in range(4):
            out[t * 4 + k, 0:32, :] = o[k * 32 : (k + 1) * 32, :]
            out[t * 4 + k, 32:40, :] = jnp.concatenate(
                [lse[t : t + 1, :], lse[4 + t : 5 + t, :], jnp.zeros((6, 128), F32)], 0
            )


def join_pair(mine, theirs):
    return pl.pallas_call(
        join_pair_kernel,
        name="join_pair",
        out_shape=jax.ShapeDtypeStruct((16, CHUNK, 128), F32),
        in_specs=[pl.BlockSpec(memory_space=pltpu.VMEM)] * 2,
        out_specs=pl.BlockSpec(memory_space=pltpu.VMEM),
        compiler_params=pltpu.CompilerParams(vmem_limit_bytes=JOIN_LIMIT),
    )(mine, theirs)


def join_plane_kernel(got, out, turned):
    rows = jnp.concatenate([got[s, 32:33, :] for s in range(16)] + [got[s, 33:34, :] for s in range(16)], 0)
    weights = []
    for h in range(2):
        part = rows[h * 16 : (h + 1) * 16, :]
        top = jnp.max(part, axis=0, keepdims=True)
        e = jnp.exp2(part - top)
        weights.append(e / jnp.sum(e, axis=0, keepdims=True))
    turned[:, 0:32] = jnp.concatenate(weights, 0).T
    start = pl.multiple_of(lax.axis_index("z") * 32, 32)
    cols = turned[pl.ds(start, 32), :]
    left = lax.broadcasted_iota(jnp.int32, (32, 128), 1) < HEAD
    o = jnp.zeros((32, 128), F32)
    for s in range(16):
        o = o + got[s, 0:32, :] * jnp.where(left, cols[:, s : s + 1], cols[:, 16 + s : 17 + s])
    out[...] = jnp.broadcast_to(o.astype(BF)[None], (64, 32, 128))


def join_plane(got):
    return pl.pallas_call(
        join_plane_kernel,
        name="join_plane",
        out_shape=jax.ShapeDtypeStruct((64, 32, 128), BF),
        in_specs=[pl.BlockSpec(memory_space=pltpu.VMEM)],
        out_specs=pl.BlockSpec(memory_space=pltpu.VMEM),
        scratch_shapes=[pltpu.VMEM((128, 128), F32)],
        compiler_params=pltpu.CompilerParams(vmem_limit_bytes=JOIN_LIMIT),
    )(got)


FB = 256


def norm(v):
    center = v - jnp.mean(v, axis=-1, keepdims=True)
    spread = jnp.mean(center * center, axis=-1, keepdims=True)
    return center * lax.rsqrt(spread + 1e-05)


def gelu(v):
    half = 0.5 * v
    return half + half * jnp.tanh(v * (0.7978845608028654 + 0.03567740813636141 * (v * v)))


def hidden_layer(ready, wup, wdown, total):
    for i in range(wup.shape[1] // FB):
        cut = slice(i * FB, (i + 1) * FB)
        total = total + mm(gelu(mm(ready, wup[:, cut])).astype(BF), wdown[cut, :])
    return total


def latent_kernel(att, lat, wo, wup, wdown, out):
    start = pl.multiple_of(lax.axis_index("c") * HALF, HALF)
    a = jnp.concatenate([att[x] for x in range(4)], 1)
    mid = lat[pl.ds(start, HALF), :].astype(F32) + mm(a, wo[...])
    out[...] = hidden_layer(norm(mid).astype(BF), wup, wdown, mid).astype(BF)


def latent(att, lat, wo, wup, wdown):
    vm = pl.BlockSpec(memory_space=pltpu.VMEM)
    return pl.pallas_call(
        latent_kernel,
        name="latent",
        out_shape=jax.ShapeDtypeStruct((HALF, D), BF),
        in_specs=[vm] * 5,
        out_specs=vm,
        compiler_params=pltpu.CompilerParams(vmem_limit_bytes=VMEM_LIMIT),
    )(att, lat, wo, wup, wdown)


DC = 512


def decode_kernel(
    tok, date, valid, table, la, lb, wq, wk, wv, wo, wup, wdown, out, kbuf, vt, qt, s0, s1, dt
):
    start = pl.multiple_of(lax.axis_index("x") * QUARTER, QUARTER)
    cut = pl.ds(start, QUARTER)
    usable = jnp.where(valid[:, cut] > 0, 1.0, 0.0).astype(F32)
    second = jnp.where(date[:, cut] == 1, 1.0, 0.0).astype(F32)
    marks = jnp.concatenate([second, usable, jnp.zeros((6, QUARTER), F32)], 0).T
    shift = jnp.where(jnp.broadcast_to(marks[:, 0:1], (QUARTER, D)) > 0.5, table[1:2, :], table[0:1, :])
    x = (tok[cut, :].astype(F32) + shift).astype(BF)
    qt[...] = mm(x, wq[...]).astype(BF).astype(F32).T.astype(BF)
    for g, ref in enumerate((la, lb)):
        rows = pl.ds(g * HALF, HALF)
        kbuf[rows, :] = mm(ref[...], wk[...]).astype(BF)
        v = mm(ref[...], wv[...]).astype(BF).astype(F32).T.astype(BF)
        for h in range(HEADS):
            vt[h, 0:HEAD, g * HALF : (g + 1) * HALF] = v[h * HEAD : (h + 1) * HEAD, :]
            vt[h, HEAD : HEAD + ONES, g * HALF : (g + 1) * HALF] = row_pick(0, (ONES, HALF)).astype(BF)
    low_start = jnp.full((8, QUARTER), -jnp.inf, F32)
    m = None
    for h in range(HEADS + 1):
        to, frm = (s0, s1) if h % 2 == 0 else (s1, s0)
        largest = low_start
        o = jnp.zeros((HEAD + ONES, QUARTER), F32)
        if h < HEADS:
            high, low = split_query(qt[h * HEAD : (h + 1) * HEAD, :])
            query = pair_query(high, low, h % 2 == 1)
            pair = h // 2 * 128
        for i in range(L // DC):
            rows = pl.ds(i * DC, DC)
            if h < HEADS:
                largest = score_step(kbuf[rows, pair : pair + 128], query, to, rows, largest)
            if h > 0:
                o = o + weight_step(vt[h - 1, :, i * DC : (i + 1) * DC], frm, rows, m)
        if h > 0:
            dt[(h - 1) * HEAD : h * HEAD, :] = o[0:HEAD, :] / o[HEAD : HEAD + 1, :]
        if h < HEADS:
            m = jnp.max(largest, axis=0, keepdims=True)
    decoded = dt[...].T.astype(BF)
    mid = x.astype(F32) + mm(decoded, wo[...])
    ready = norm(mid).astype(BF)
    result = hidden_layer(ready, wup, wdown, jnp.zeros((QUARTER, C), F32))
    out[...] = jnp.where(jnp.broadcast_to(marks[:, 1:2], (QUARTER, C)) > 0.5, result, 0.0)


def decode(tok, date, valid, table, la, lb, wq, wk, wv, wo, wup, wdown):
    vm = pl.BlockSpec(memory_space=pltpu.VMEM)
    return pl.pallas_call(
        decode_kernel,
        name="decode",
        out_shape=jax.ShapeDtypeStruct((QUARTER, C), F32),
        in_specs=[vm] * 12,
        out_specs=vm,
        scratch_shapes=[
            pltpu.VMEM((L, D), BF),
            pltpu.VMEM((HEADS, HEAD + ONES, L), BF),
            pltpu.VMEM((D, QUARTER), BF),
            pltpu.VMEM((L, QUARTER), F32),
            pltpu.VMEM((L, QUARTER), F32),
            pltpu.VMEM((D, QUARTER), F32),
        ],
        compiler_params=pltpu.CompilerParams(vmem_limit_bytes=VMEM_LIMIT),
    )(tok, date, valid, table, la, lb, wq, wk, wv, wo, wup, wdown)


def per_device(
    tokens,
    date_index,
    valid,
    date_table,
    latents,
    wq_enc,
    wk_enc,
    wv_enc,
    wo_enc,
    w_lat_up,
    w_lat_down,
    wq_dec,
    wk_dec,
    wv_dec,
    wo_dec,
    w_out_up,
    w_out_down,
):
    date = date_index.reshape(1, TOK)
    flag = valid.reshape(1, TOK)
    swap = [(0, 1), (1, 0)]
    keep, send = encode(tokens, date, flag, date_table, latents, wq_enc, wk_enc, wv_enc)
    other = lax.ppermute(send, "c", swap)
    chunks = join_pair(keep, other)
    got = lax.all_to_all(chunks, ("y", "z"), 0, 0)
    copies = join_plane(got)
    attended = lax.all_to_all(copies, ("x", "y", "z"), 0, 0).reshape(4, HALF, 128)
    own = latent(attended, latents, wo_enc, w_lat_up, w_lat_down)
    others = lax.ppermute(own, "c", swap)
    return decode(
        tokens, date, flag, date_table, own, others,
        wq_dec, wk_dec, wv_dec, wo_dec, w_out_up, w_out_down,
    )


def solution(mesh):
    parts = Mesh(mesh.devices.reshape(4, 4, 4, 2), ("x", "y", "z", "c"))
    tok = ("y", "z", "c")
    in_specs = (
        P(tok, None),
        P(tok),
        P(tok),
        P(),
        P(),
        P(None, "x"),
        P(None, "x"),
        P(None, "x"),
        P(),
        P(),
        P(),
        P(),
        P(),
        P(),
        P(),
        P(),
        P(),
    )
    out_specs = P((*tok, "x"), None)
    return jax.shard_map(
        per_device, mesh=parts, in_specs=in_specs, out_specs=out_specs, check_vma=False
    )
```

```python
import functools

import jax
import jax.numpy as jnp
from jax import lax
from jax.experimental import pallas as pl
from jax.experimental.pallas import tpu as pltpu
from jax.sharding import Mesh, PartitionSpec as P

D = 512
HEADS = 8
HEAD = 64
L = 1024
HALF = 512
TOK = 2048
QUARTER = 512
F = 2048
C = 128
SCALE = HEAD ** (-0.5)
LOG2E = 1.4426950408889634
NEG = -1e30
PAY = HALF + 8
CHUNK = 40
BF = jnp.bfloat16
F32 = jnp.float32
VMEM_LIMIT = 20 * 1024 * 1024
JOIN_LIMIT = 8 * 1024 * 1024


def mm(a, b):
    return jnp.dot(a, b, preferred_element_type=F32)


def row_pick(row, shape):
    return jnp.where(lax.broadcasted_iota(jnp.int32, shape, 0) == row, 1.0, 0.0).astype(F32)


EC = 512
EB = 256
ES = 512
ONES = 16


def hbm(*arrays):
    return [pltpu.with_memory_space_constraint(a, pltpu.HBM) for a in arrays]


def fetch(pairs, sems):
    copies = [pltpu.make_async_copy(a, b, sems.at[i]) for i, (a, b) in enumerate(pairs)]
    for copy in copies:
        copy.start()
    return copies


def split_query(q):
    scaled = q.astype(F32) * (SCALE * LOG2E)
    high = scaled.astype(BF)
    return high, (scaled - high.astype(F32)).astype(BF)


def pair_query(high, low, odd):
    zero = jnp.zeros(high.shape, BF)
    rows = [zero, high, zero, low] if odd else [high, zero, low, zero]
    return jnp.concatenate(rows, 0)


def score_step(keys, query, to, rows, largest):
    s = mm(jnp.concatenate([keys, keys], 1), query)
    to[rows, :] = s
    return jnp.maximum(largest, jnp.max(s.reshape(s.shape[0] // 8, 8, s.shape[1]), axis=0))


def weight_step(values, frm, rows, m):
    return mm(values, jnp.exp2(frm[rows, :] - m).astype(BF))


def encode_kernel(
    tok_h, date_h, valid_h, table_h, lat_h, wq_h, wk_h, wv_h, keep, send,
    tok, date, valid, table, lat, wq, wkv, kbuf, vt, qbuf, s0, s1, sems,
):
    c = lax.axis_index("c")
    pairs = [(wq_h, wq), (lat_h, lat), (date_h, date), (valid_h, valid), (table_h, table)]
    pairs += [(wk_h, wkv.at[:, 0:128]), (wv_h, wkv.at[:, 128:256]), (tok_h, tok)]
    copies = fetch(pairs, sems)
    copies[0].wait()
    copies[1].wait()
    for half in range(2):
        start = pl.multiple_of((1 - c if half == 0 else c) * HALF, HALF)
        q = mm(lat[pl.ds(start, HALF), :], wq[...]).astype(BF).astype(F32)
        qt = q.T.astype(BF)
        for j in range(HALF // EB):
            high, low = split_query(qt[:, j * EB : (j + 1) * EB])
            for h in range(2):
                own = slice(h * HEAD, (h + 1) * HEAD)
                qbuf[(half * 2 + j) * 2 + h] = pair_query(high[own], low[own], h == 1)
    for copy in copies[2:]:
        copy.wait()
    usable = jnp.where(valid[...] > 0, 1.0, 0.0).astype(F32)
    second = jnp.where(date[...] == 1, 1.0, 0.0).astype(F32)
    flags = jnp.concatenate([second, usable, jnp.zeros((6, TOK), F32)], 0)
    row0, row1 = table[0:1, :], table[1:2, :]
    for h in range(2):
        vt[h, HEAD : HEAD + ONES, :] = jnp.concatenate([usable, jnp.zeros((ONES - 1, TOK), F32)], 0).astype(BF)
    for i in range(TOK // EC):
        rows = pl.ds(i * EC, EC)
        cols = slice(i * EC, (i + 1) * EC)
        marks = flags[:, cols].T
        shift = jnp.where(jnp.broadcast_to(marks[:, 0:1], (EC, D)) > 0.5, row1, row0)
        x = (tok[rows, :].astype(F32) + shift).astype(BF)
        kv = mm(x, wkv[...])
        k = kv[:, 0:128]
        first = jnp.broadcast_to(k.reshape(EC // 16, 16, 128)[:, 0:1, :], (EC // 16, 16, 128)).reshape(EC, 128)
        kbuf[rows, :] = jnp.where(jnp.broadcast_to(marks[:, 1:2], (EC, 128)) > 0.5, k, first).astype(BF)
        v = (kv[:, 128:256].astype(BF).astype(F32).T * usable[:, cols]).astype(BF)
        vt[0, 0:HEAD, cols] = v[0:HEAD]
        vt[1, 0:HEAD, cols] = v[HEAD:128]

    low_start = jnp.full((8, EB), -jnp.inf, F32)
    blocks = 2 * L // EB

    def step(n, frm, to, m, odd, score, weigh):
        largest = low_start
        o = jnp.zeros((HEAD + ONES, EB), F32)
        for i in range(TOK // ES):
            rows = pl.ds(i * ES, ES)
            if score:
                largest = score_step(kbuf[rows, :], qbuf[n + 1], to, rows, largest)
            if weigh:
                o = o + weight_step(vt[odd, :, i * ES : (i + 1) * ES], frm, rows, m)
        t = o[HEAD : HEAD + 1, :]
        return jnp.max(largest, axis=0, keepdims=True), o[0:HEAD, :] / t if weigh else None, m + jnp.log2(t)

    def put(to, j, o0, o1, l0, l1):
        to[pl.ds(pl.multiple_of(j * EB, EB), EB), :] = jnp.concatenate([o0, o1], 0).T
        for h, line in enumerate((l0, l1)):
            for k in range(EB // 128):
                to[pl.ds(HALF + h * 4 + j * (EB // 128) + k, 1), :] = line[:, k * 128 : (k + 1) * 128]

    m, _, _ = step(-1, s1, s0, jnp.zeros((1, EB), F32), 0, True, False)
    for j in range(L // EB):
        to = send if j < HALF // EB else keep
        m, o0, l0 = step(2 * j, s0, s1, m, 0, True, True)
        m, o1, l1 = step(2 * j + 1, s1, s0, m, 1, j < L // EB - 1, True)
        put(to, j % (HALF // EB), o0, o1, l0, l1)


def encode(tok, date, valid, table, lat, wq, wk, wv):
    blocks = 2 * L // EB
    vm = pl.BlockSpec(memory_space=pltpu.VMEM)
    return pl.pallas_call(
        encode_kernel,
        name="encode",
        out_shape=(jax.ShapeDtypeStruct((PAY, 128), F32),) * 2,
        in_specs=[pl.BlockSpec(memory_space=pltpu.HBM)] * 8,
        out_specs=(vm, vm),
        scratch_shapes=[
            pltpu.VMEM((TOK, D), BF),
            pltpu.VMEM((1, TOK), jnp.int32),
            pltpu.VMEM((1, TOK), jnp.int32),
            pltpu.VMEM((2, D), F32),
            pltpu.VMEM((L, D), BF),
            pltpu.VMEM((D, 128), BF),
            pltpu.VMEM((D, 256), BF),
            pltpu.VMEM((TOK, 128), BF),
            pltpu.VMEM((2, HEAD + ONES, TOK), BF),
            pltpu.VMEM((blocks, 256, EB), BF),
            pltpu.VMEM((TOK, EB), F32),
            pltpu.VMEM((TOK, EB), F32),
            pltpu.SemaphoreType.DMA((8,)),
        ],
        compiler_params=pltpu.CompilerParams(vmem_limit_bytes=VMEM_LIMIT),
        cost_estimate=pl.CostEstimate(
            flops=2 * TOK * D * 256 + 4 * 2 * L * TOK * HEAD + 2 * L * D * 128,
            bytes_accessed=4 << 20,
            transcendentals=2 * L * TOK,
        ),
    )(*hbm(tok, date, valid, table, lat, wq, wk, wv))


def join_pair_kernel(mine, theirs, out):
    a, b = mine[HALF:PAY, :], theirs[HALF:PAY, :]
    top = jnp.maximum(a, b)
    ea, eb = jnp.exp2(a - top), jnp.exp2(b - top)
    total = ea + eb
    lse = top + jnp.log2(total)
    wa, wb = (ea / total).T, (eb / total).T
    left = lax.broadcasted_iota(jnp.int32, (128, 128), 1) < HEAD
    for t in range(4):
        fa = jnp.where(left, wa[:, t : t + 1], wa[:, 4 + t : 5 + t])
        fb = jnp.where(left, wb[:, t : t + 1], wb[:, 4 + t : 5 + t])
        rows = pl.ds(t * 128, 128)
        o = mine[rows, :] * fa + theirs[rows, :] * fb
        for k in range(4):
            out[t * 4 + k, 0:32, :] = o[k * 32 : (k + 1) * 32, :]
            out[t * 4 + k, 32:40, :] = jnp.concatenate(
                [lse[t : t + 1, :], lse[4 + t : 5 + t, :], jnp.zeros((6, 128), F32)], 0
            )


def join_pair(mine, theirs):
    return pl.pallas_call(
        join_pair_kernel,
        name="join_pair",
        out_shape=jax.ShapeDtypeStruct((16, CHUNK, 128), F32),
        in_specs=[pl.BlockSpec(memory_space=pltpu.VMEM)] * 2,
        out_specs=pl.BlockSpec(memory_space=pltpu.VMEM),
        compiler_params=pltpu.CompilerParams(vmem_limit_bytes=JOIN_LIMIT),
    )(mine, theirs)


def join_plane_kernel(got, out, turned):
    rows = jnp.concatenate([got[s, 32:33, :] for s in range(16)] + [got[s, 33:34, :] for s in range(16)], 0)
    weights = []
    for h in range(2):
        part = rows[h * 16 : (h + 1) * 16, :]
        top = jnp.max(part, axis=0, keepdims=True)
        e = jnp.exp2(part - top)
        weights.append(e / jnp.sum(e, axis=0, keepdims=True))
    turned[:, 0:32] = jnp.concatenate(weights, 0).T
    start = pl.multiple_of(lax.axis_index("z") * 32, 32)
    cols = turned[pl.ds(start, 32), :]
    left = lax.broadcasted_iota(jnp.int32, (32, 128), 1) < HEAD
    o = jnp.zeros((32, 128), F32)
    for s in range(16):
        o = o + got[s, 0:32, :] * jnp.where(left, cols[:, s : s + 1], cols[:, 16 + s : 17 + s])
    out[...] = jnp.broadcast_to(o.astype(BF)[None], (64, 32, 128))


def join_plane(got):
    return pl.pallas_call(
        join_plane_kernel,
        name="join_plane",
        out_shape=jax.ShapeDtypeStruct((64, 32, 128), BF),
        in_specs=[pl.BlockSpec(memory_space=pltpu.VMEM)],
        out_specs=pl.BlockSpec(memory_space=pltpu.VMEM),
        scratch_shapes=[pltpu.VMEM((128, 128), F32)],
        compiler_params=pltpu.CompilerParams(vmem_limit_bytes=JOIN_LIMIT),
    )(got)


def norm(v):
    center = v - jnp.mean(v, axis=-1, keepdims=True)
    spread = jnp.mean(center * center, axis=-1, keepdims=True)
    return center * lax.rsqrt(spread + 1e-05)


def gelu(v):
    half = 0.5 * v
    return half + half * jnp.tanh(v * (0.7978845608028654 + 0.03567740813636141 * (v * v)))


def hidden_layer(ready, wup, wdown, total, width):
    for i in range(F // width):
        cut = slice(i * width, (i + 1) * width)
        total = total + mm(gelu(mm(ready, wup[:, cut])).astype(BF), wdown[cut, :])
    return total


def latent_kernel(att, lat, wo, wup, wdown, out):
    start = pl.multiple_of(lax.axis_index("c") * HALF, HALF)
    a = jnp.concatenate([att[x] for x in range(4)], 1)
    mid = lat[pl.ds(start, HALF), :].astype(F32) + mm(a, wo[...])
    out[...] = hidden_layer(norm(mid).astype(BF), wup, wdown, mid, 256).astype(BF)


def latent(att, lat, wo, wup, wdown):
    vm = pl.BlockSpec(memory_space=pltpu.VMEM)
    return pl.pallas_call(
        latent_kernel,
        name="latent",
        out_shape=jax.ShapeDtypeStruct((HALF, D), BF),
        in_specs=[vm] * 5,
        out_specs=vm,
        compiler_params=pltpu.CompilerParams(vmem_limit_bytes=VMEM_LIMIT),
    )(att, lat, wo, wup, wdown)


def ask_kernel(tok, date, table, wq, x, qt):
    cut = pl.ds(pl.multiple_of(lax.axis_index("x") * QUARTER, QUARTER), QUARTER)
    second = jnp.where(date[:, cut] == 1, 1.0, 0.0).astype(F32)
    marks = jnp.concatenate([second, jnp.zeros((7, QUARTER), F32)], 0).T
    shift = jnp.where(jnp.broadcast_to(marks[:, 0:1], (QUARTER, D)) > 0.5, table[1:2, :], table[0:1, :])
    own = (tok[cut, :].astype(F32) + shift).astype(BF)
    x[...] = own
    qt[...] = mm(own, wq[...]).astype(BF).astype(F32).T.astype(BF)


def ask(tok, date, table, wq):
    vm = pl.BlockSpec(memory_space=pltpu.VMEM)
    return pl.pallas_call(
        ask_kernel,
        name="ask",
        out_shape=(jax.ShapeDtypeStruct((QUARTER, D), BF), jax.ShapeDtypeStruct((D, QUARTER), BF)),
        in_specs=[vm] * 4,
        out_specs=(vm, vm),
        compiler_params=pltpu.CompilerParams(vmem_limit_bytes=JOIN_LIMIT),
        cost_estimate=pl.CostEstimate(flops=2 * QUARTER * D * D, bytes_accessed=2 << 20, transcendentals=0),
    )(tok, date, table, wq)


def half_kernel(latents, wk, wv, keys, values):
    k = mm(latents[...], wk[...]).astype(BF)
    for pair in range(HEADS // 2):
        keys[pair] = k[:, pair * 128 : (pair + 1) * 128]
    v = mm(latents[...], wv[...]).astype(BF).astype(F32).T.astype(BF)
    ones = row_pick(0, (ONES, HALF)).astype(BF)
    for h in range(HEADS):
        values[h] = jnp.concatenate([v[h * HEAD : (h + 1) * HEAD], ones], 0)


KEYS = (HEADS // 2, HALF, 128)
VALUES = (HEADS, HEAD + ONES, HALF)


def half(latents, wk, wv):
    vm = pl.BlockSpec(memory_space=pltpu.VMEM)
    return pl.pallas_call(
        half_kernel,
        name="half",
        out_shape=(jax.ShapeDtypeStruct(KEYS, BF), jax.ShapeDtypeStruct(VALUES, BF)),
        in_specs=[vm] * 3,
        out_specs=(vm, vm),
        compiler_params=pltpu.CompilerParams(vmem_limit_bytes=JOIN_LIMIT),
        cost_estimate=pl.CostEstimate(flops=4 * HALF * D * D, bytes_accessed=3 << 20, transcendentals=0),
    )(latents, wk, wv)


def decode_kernel(x, qt, valid, keys, values, lb, wk, wv, wo, wup, wdown, out, keys2, values2, s0, s1, dt):
    half_kernel(lb, wk, wv, keys2, values2)
    low_start = jnp.full((8, QUARTER), -jnp.inf, F32)
    m = None
    for h in range(HEADS + 1):
        to, frm = (s0, s1) if h % 2 == 0 else (s1, s0)
        largest = low_start
        o = jnp.zeros((HEAD + ONES, QUARTER), F32)
        if h < HEADS:
            high, low = split_query(qt[h * HEAD : (h + 1) * HEAD, :])
            query = pair_query(high, low, h % 2 == 1)
        for i, (k, v) in enumerate(((keys, values), (keys2, values2))):
            rows = pl.ds(i * HALF, HALF)
            if h < HEADS:
                largest = score_step(k[h // 2], query, to, rows, largest)
            if h > 0:
                o = o + weight_step(v[h - 1], frm, rows, m)
        if h > 0:
            dt[(h - 1) * HEAD : h * HEAD, :] = o[0:HEAD, :] / o[HEAD : HEAD + 1, :]
        if h < HEADS:
            m = jnp.max(largest, axis=0, keepdims=True)
    decoded = dt[...].T.astype(BF)
    mid = x[...].astype(F32) + mm(decoded, wo[...])
    ready = norm(mid).astype(BF)
    result = hidden_layer(ready, wup, wdown, jnp.zeros((QUARTER, C), F32), 512)
    cut = pl.ds(pl.multiple_of(lax.axis_index("x") * QUARTER, QUARTER), QUARTER)
    usable = jnp.where(valid[:, cut] > 0, 1.0, 0.0).astype(F32)
    marks = jnp.concatenate([usable, jnp.zeros((7, QUARTER), F32)], 0).T
    out[...] = jnp.where(jnp.broadcast_to(marks[:, 0:1], (QUARTER, C)) > 0.5, result, 0.0)


def decode(x, qt, valid, keys, values, lb, wk, wv, wo, wup, wdown):
    vm = pl.BlockSpec(memory_space=pltpu.VMEM)
    return pl.pallas_call(
        decode_kernel,
        name="decode",
        out_shape=jax.ShapeDtypeStruct((QUARTER, C), F32),
        in_specs=[vm] * 11,
        out_specs=vm,
        scratch_shapes=[
            pltpu.VMEM(KEYS, BF),
            pltpu.VMEM(VALUES, BF),
            pltpu.VMEM((L, QUARTER), F32),
            pltpu.VMEM((L, QUARTER), F32),
            pltpu.VMEM((D, QUARTER), F32),
        ],
        compiler_params=pltpu.CompilerParams(vmem_limit_bytes=VMEM_LIMIT),
    )(x, qt, valid, keys, values, lb, wk, wv, wo, wup, wdown)


def per_device(
    tokens,
    date_index,
    valid,
    date_table,
    latents,
    wq_enc,
    wk_enc,
    wv_enc,
    wo_enc,
    w_lat_up,
    w_lat_down,
    wq_dec,
    wk_dec,
    wv_dec,
    wo_dec,
    w_out_up,
    w_out_down,
):
    date = date_index.reshape(1, TOK)
    flag = valid.reshape(1, TOK)
    swap = [(0, 1), (1, 0)]
    keep, send = encode(tokens, date, flag, date_table, latents, wq_enc, wk_enc, wv_enc)
    other = lax.ppermute(send, "c", swap)
    chunks = join_pair(keep, other)
    got = lax.all_to_all(chunks, ("y", "z"), 0, 0)
    copies = join_plane(got)
    attended = lax.all_to_all(copies, ("x", "y", "z"), 0, 0).reshape(4, HALF, 128)
    own = latent(attended, latents, wo_enc, w_lat_up, w_lat_down)
    others = lax.ppermute(own, "c", swap)
    x, queries = ask(tokens, date, date_table, wq_dec)
    keys, values = half(own, wk_dec, wv_dec)
    return decode(x, queries, flag, keys, values, others, wk_dec, wv_dec, wo_dec, w_out_up, w_out_down)


def solution(mesh):
    parts = Mesh(mesh.devices.reshape(4, 4, 4, 2), ("x", "y", "z", "c"))
    tok = ("y", "z", "c")
    in_specs = (
        P(tok, None),
        P(tok),
        P(tok),
        P(),
        P(),
        P(None, "x"),
        P(None, "x"),
        P(None, "x"),
        P(),
        P(),
        P(),
        P(),
        P(),
        P(),
        P(),
        P(),
        P(),
    )
    out_specs = P((*tok, "x"), None)
    return jax.shard_map(
        per_device, mesh=parts, in_specs=in_specs, out_specs=out_specs, check_vma=False
    )
```

```python
import functools

import jax
import jax.numpy as jnp
from jax import lax
from jax.experimental import pallas as pl
from jax.experimental.pallas import tpu as pltpu
from jax.sharding import Mesh, PartitionSpec as P

D = 512
HEADS = 8
HEAD = 64
L = 1024
HALF = 512
TOK = 2048
QUARTER = 512
F = 2048
C = 128
SCALE = HEAD ** (-0.5)
LOG2E = 1.4426950408889634
PAY = HALF + 8
CHUNK = 40
BF = jnp.bfloat16
F32 = jnp.float32
VMEM_LIMIT = 20 * 1024 * 1024
JOIN_LIMIT = 8 * 1024 * 1024


def mm(a, b):
    return jnp.dot(a, b, preferred_element_type=F32)


def row_pick(row, shape):
    return jnp.where(lax.broadcasted_iota(jnp.int32, shape, 0) == row, 1.0, 0.0).astype(F32)


EC = 512
EB = 256
ES = 512
ONES = 16


def hbm(*arrays):
    return [pltpu.with_memory_space_constraint(a, pltpu.HBM) for a in arrays]


def fetch(pairs, sems):
    copies = [pltpu.make_async_copy(a, b, sems.at[i]) for i, (a, b) in enumerate(pairs)]
    for copy in copies:
        copy.start()
    return copies


def split_query(q):
    scaled = q.astype(F32) * (SCALE * LOG2E)
    high = scaled.astype(BF)
    return high, (scaled - high.astype(F32)).astype(BF)


def pair_query(high, low, odd):
    zero = jnp.zeros(high.shape, BF)
    rows = [zero, high, zero, low] if odd else [high, zero, low, zero]
    return jnp.concatenate(rows, 0)


def score_step(keys, query, to, rows, largest):
    s = mm(jnp.concatenate([keys, keys], 1), query)
    to[rows, :] = s
    return jnp.maximum(largest, jnp.max(s.reshape(s.shape[0] // 8, 8, s.shape[1]), axis=0))


def weight_step(values, frm, rows, m):
    return mm(values, jnp.exp2(frm[rows, :] - m).astype(BF))


def encode_kernel(
    tok_h, date_h, valid_h, table_h, lat_h, wq_h, wk_h, wv_h, keep, send,
    tok, date, valid, table, lat, wq, wkv, kbuf, vt, qbuf, s0, s1, sems,
):
    c = lax.axis_index("c")
    pairs = [(wq_h, wq), (lat_h, lat), (date_h, date), (valid_h, valid), (table_h, table)]
    pairs += [(wk_h, wkv.at[:, 0:128]), (wv_h, wkv.at[:, 128:256])]
    pairs += [(tok_h.at[pl.ds(i * EC, EC)], tok.at[pl.ds(i * EC, EC)]) for i in range(TOK // EC)]
    copies = fetch(pairs, sems)
    copies[0].wait()
    copies[1].wait()
    for half in range(2):
        start = pl.multiple_of((1 - c if half == 0 else c) * HALF, HALF)
        q = mm(lat[pl.ds(start, HALF), :], wq[...]).astype(BF).astype(F32)
        qt = q.T.astype(BF)
        for j in range(HALF // EB):
            high, low = split_query(qt[:, j * EB : (j + 1) * EB])
            for h in range(2):
                own = slice(h * HEAD, (h + 1) * HEAD)
                qbuf[(half * 2 + j) * 2 + h] = pair_query(high[own], low[own], h == 1)
    for copy in copies[2:]:
        copy.wait()
    usable = jnp.where(valid[...] > 0, 1.0, 0.0).astype(F32)
    second = jnp.where(date[...] == 1, 1.0, 0.0).astype(F32)
    flags = jnp.concatenate([second, usable, jnp.zeros((6, TOK), F32)], 0)
    row0, row1 = table[0:1, :], table[1:2, :]
    for h in range(2):
        vt[h, HEAD : HEAD + ONES, :] = jnp.concatenate([usable, jnp.zeros((ONES - 1, TOK), F32)], 0).astype(BF)
    for i in range(TOK // EC):
        rows = pl.ds(i * EC, EC)
        cols = slice(i * EC, (i + 1) * EC)
        marks = flags[:, cols].T
        shift = jnp.where(jnp.broadcast_to(marks[:, 0:1], (EC, D)) > 0.5, row1, row0)
        x = (tok[rows, :].astype(F32) + shift).astype(BF)
        kv = mm(x, wkv[...])
        k = kv[:, 0:128]
        first = jnp.broadcast_to(k.reshape(EC // 16, 16, 128)[:, 0:1, :], (EC // 16, 16, 128)).reshape(EC, 128)
        kbuf[rows, :] = jnp.where(jnp.broadcast_to(marks[:, 1:2], (EC, 128)) > 0.5, k, first).astype(BF)
        v = (kv[:, 128:256].astype(BF).astype(F32).T * usable[:, cols]).astype(BF)
        vt[0, 0:HEAD, cols] = v[0:HEAD]
        vt[1, 0:HEAD, cols] = v[HEAD:128]

    low_start = jnp.full((8, EB), -jnp.inf, F32)
    blocks = 2 * L // EB

    def step(n, frm, to, m, odd, score, weigh):
        largest = low_start
        o = jnp.zeros((HEAD + ONES, EB), F32)
        for i in range(TOK // ES):
            rows = pl.ds(i * ES, ES)
            if score:
                largest = score_step(kbuf[rows, :], qbuf[n + 1], to, rows, largest)
            if weigh:
                o = o + weight_step(vt[odd, :, i * ES : (i + 1) * ES], frm, rows, m)
        t = o[HEAD : HEAD + 1, :]
        return jnp.max(largest, axis=0, keepdims=True), o[0:HEAD, :] / t if weigh else None, m + jnp.log2(t)

    def put(to, j, o0, o1, l0, l1):
        to[pl.ds(pl.multiple_of(j * EB, EB), EB), :] = jnp.concatenate([o0, o1], 0).T
        for h, line in enumerate((l0, l1)):
            for k in range(EB // 128):
                to[pl.ds(HALF + h * 4 + j * (EB // 128) + k, 1), :] = line[:, k * 128 : (k + 1) * 128]

    m, _, _ = step(-1, s1, s0, jnp.zeros((1, EB), F32), 0, True, False)
    for j in range(L // EB):
        to = send if j < HALF // EB else keep
        m, o0, l0 = step(2 * j, s0, s1, m, 0, True, True)
        m, o1, l1 = step(2 * j + 1, s1, s0, m, 1, j < L // EB - 1, True)
        put(to, j % (HALF // EB), o0, o1, l0, l1)


def encode(tok, date, valid, table, lat, wq, wk, wv):
    blocks = 2 * L // EB
    vm = pl.BlockSpec(memory_space=pltpu.VMEM)
    return pl.pallas_call(
        encode_kernel,
        name="encode",
        out_shape=(jax.ShapeDtypeStruct((PAY, 128), F32),) * 2,
        in_specs=[pl.BlockSpec(memory_space=pltpu.HBM)] * 8,
        out_specs=(vm, vm),
        scratch_shapes=[
            pltpu.VMEM((TOK, D), BF),
            pltpu.VMEM((1, TOK), jnp.int32),
            pltpu.VMEM((1, TOK), jnp.int32),
            pltpu.VMEM((2, D), F32),
            pltpu.VMEM((L, D), BF),
            pltpu.VMEM((D, 128), BF),
            pltpu.VMEM((D, 256), BF),
            pltpu.VMEM((TOK, 128), BF),
            pltpu.VMEM((2, HEAD + ONES, TOK), BF),
            pltpu.VMEM((blocks, 256, EB), BF),
            pltpu.VMEM((TOK, EB), F32),
            pltpu.VMEM((TOK, EB), F32),
            pltpu.SemaphoreType.DMA((7 + TOK // EC,)),
        ],
        compiler_params=pltpu.CompilerParams(vmem_limit_bytes=VMEM_LIMIT),
        cost_estimate=pl.CostEstimate(
            flops=2 * TOK * D * 256 + 4 * 2 * L * TOK * HEAD + 2 * L * D * 128,
            bytes_accessed=4 << 20,
            transcendentals=2 * L * TOK,
        ),
    )(*hbm(tok, date, valid, table, lat, wq, wk, wv))


def join_pair_kernel(mine, theirs, out):
    a, b = mine[HALF:PAY, :], theirs[HALF:PAY, :]
    top = jnp.maximum(a, b)
    ea, eb = jnp.exp2(a - top), jnp.exp2(b - top)
    total = ea + eb
    lse = top + jnp.log2(total)
    wa, wb = (ea / total).T, (eb / total).T
    left = lax.broadcasted_iota(jnp.int32, (128, 128), 1) < HEAD
    for t in range(4):
        fa = jnp.where(left, wa[:, t : t + 1], wa[:, 4 + t : 5 + t])
        fb = jnp.where(left, wb[:, t : t + 1], wb[:, 4 + t : 5 + t])
        rows = pl.ds(t * 128, 128)
        o = mine[rows, :] * fa + theirs[rows, :] * fb
        for k in range(4):
            out[t * 4 + k, 0:32, :] = o[k * 32 : (k + 1) * 32, :]
            out[t * 4 + k, 32:40, :] = jnp.concatenate(
                [lse[t : t + 1, :], lse[4 + t : 5 + t, :], jnp.zeros((6, 128), F32)], 0
            )


def join_pair(mine, theirs):
    return pl.pallas_call(
        join_pair_kernel,
        name="join_pair",
        out_shape=jax.ShapeDtypeStruct((16, CHUNK, 128), F32),
        in_specs=[pl.BlockSpec(memory_space=pltpu.VMEM)] * 2,
        out_specs=pl.BlockSpec(memory_space=pltpu.VMEM),
        compiler_params=pltpu.CompilerParams(vmem_limit_bytes=JOIN_LIMIT),
    )(mine, theirs)


def join_plane_kernel(got, out, turned):
    rows = jnp.concatenate([got[s, 32:33, :] for s in range(16)] + [got[s, 33:34, :] for s in range(16)], 0)
    weights = []
    for h in range(2):
        part = rows[h * 16 : (h + 1) * 16, :]
        top = jnp.max(part, axis=0, keepdims=True)
        e = jnp.exp2(part - top)
        weights.append(e / jnp.sum(e, axis=0, keepdims=True))
    turned[:, 0:32] = jnp.concatenate(weights, 0).T
    start = pl.multiple_of(lax.axis_index("y") * 32, 32)
    cols = turned[pl.ds(start, 32), :]
    left = lax.broadcasted_iota(jnp.int32, (32, 128), 1) < HEAD
    o = jnp.zeros((32, 128), F32)
    for s in range(16):
        o = o + got[s, 0:32, :] * jnp.where(left, cols[:, s : s + 1], cols[:, 16 + s : 17 + s])
    out[...] = jnp.broadcast_to(o.astype(BF)[None], (64, 32, 128))


def join_plane(got):
    return pl.pallas_call(
        join_plane_kernel,
        name="join_plane",
        out_shape=jax.ShapeDtypeStruct((64, 32, 128), BF),
        in_specs=[pl.BlockSpec(memory_space=pltpu.VMEM)],
        out_specs=pl.BlockSpec(memory_space=pltpu.VMEM),
        scratch_shapes=[pltpu.VMEM((128, 128), F32)],
        compiler_params=pltpu.CompilerParams(vmem_limit_bytes=JOIN_LIMIT),
    )(got)


def norm(v):
    center = v - jnp.mean(v, axis=-1, keepdims=True)
    spread = jnp.mean(center * center, axis=-1, keepdims=True)
    return center * lax.rsqrt(spread + 1e-05)


def gelu(v):
    half = 0.5 * v
    return half + half * jnp.tanh(v * (0.7978845608028654 + 0.03567740813636141 * (v * v)))


def hidden_layer(ready, wup, wdown, total, width):
    for i in range(F // width):
        cut = slice(i * width, (i + 1) * width)
        total = total + mm(gelu(mm(ready, wup[:, cut])).astype(BF), wdown[cut, :])
    return total


def latent_kernel(att, lat, wo, wup, wdown, out):
    start = pl.multiple_of(lax.axis_index("c") * HALF, HALF)
    a = jnp.concatenate([jnp.concatenate([att[z, x] for z in range(4)], 0) for x in range(4)], 1)
    mid = lat[pl.ds(start, HALF), :].astype(F32) + mm(a, wo[...])
    out[...] = hidden_layer(norm(mid).astype(BF), wup, wdown, mid, 256).astype(BF)


def latent(att, lat, wo, wup, wdown):
    vm = pl.BlockSpec(memory_space=pltpu.VMEM)
    return pl.pallas_call(
        latent_kernel,
        name="latent",
        out_shape=jax.ShapeDtypeStruct((HALF, D), BF),
        in_specs=[vm] * 5,
        out_specs=vm,
        compiler_params=pltpu.CompilerParams(vmem_limit_bytes=VMEM_LIMIT),
    )(att, lat, wo, wup, wdown)


def ask_kernel(tok, date, table, wq, x, qt):
    cut = pl.ds(pl.multiple_of(lax.axis_index("x") * QUARTER, QUARTER), QUARTER)
    second = jnp.where(date[:, cut] == 1, 1.0, 0.0).astype(F32)
    marks = jnp.concatenate([second, jnp.zeros((7, QUARTER), F32)], 0).T
    shift = jnp.where(jnp.broadcast_to(marks[:, 0:1], (QUARTER, D)) > 0.5, table[1:2, :], table[0:1, :])
    own = (tok[cut, :].astype(F32) + shift).astype(BF)
    x[...] = own
    qt[...] = mm(own, wq[...]).astype(BF).astype(F32).T.astype(BF)


def ask(tok, date, table, wq):
    vm = pl.BlockSpec(memory_space=pltpu.VMEM)
    return pl.pallas_call(
        ask_kernel,
        name="ask",
        out_shape=(jax.ShapeDtypeStruct((QUARTER, D), BF), jax.ShapeDtypeStruct((D, QUARTER), BF)),
        in_specs=[vm] * 4,
        out_specs=(vm, vm),
        compiler_params=pltpu.CompilerParams(vmem_limit_bytes=JOIN_LIMIT),
        cost_estimate=pl.CostEstimate(flops=2 * QUARTER * D * D, bytes_accessed=2 << 20, transcendentals=0),
    )(tok, date, table, wq)


def half_kernel(latents, wk, wv, keys, values):
    k = mm(latents[...], wk[...]).astype(BF)
    for pair in range(HEADS // 2):
        keys[pair] = k[:, pair * 128 : (pair + 1) * 128]
    v = mm(latents[...], wv[...]).astype(BF).astype(F32).T.astype(BF)
    ones = row_pick(0, (ONES, HALF)).astype(BF)
    for h in range(HEADS):
        values[h] = jnp.concatenate([v[h * HEAD : (h + 1) * HEAD], ones], 0)


KEYS = (HEADS // 2, HALF, 128)
VALUES = (HEADS, HEAD + ONES, HALF)


def half(latents, wk, wv):
    vm = pl.BlockSpec(memory_space=pltpu.VMEM)
    return pl.pallas_call(
        half_kernel,
        name="half",
        out_shape=(jax.ShapeDtypeStruct(KEYS, BF), jax.ShapeDtypeStruct(VALUES, BF)),
        in_specs=[vm] * 3,
        out_specs=(vm, vm),
        compiler_params=pltpu.CompilerParams(vmem_limit_bytes=JOIN_LIMIT),
        cost_estimate=pl.CostEstimate(flops=4 * HALF * D * D, bytes_accessed=3 << 20, transcendentals=0),
    )(latents, wk, wv)


def decode_kernel(x, qt, valid, keys, values, lb, wk, wv, wo, wup, wdown, out, keys2, values2, s0, s1, dt):
    half_kernel(lb, wk, wv, keys2, values2)
    low_start = jnp.full((8, QUARTER), -jnp.inf, F32)
    m = None
    for h in range(HEADS + 1):
        to, frm = (s0, s1) if h % 2 == 0 else (s1, s0)
        largest = low_start
        o = jnp.zeros((HEAD + ONES, QUARTER), F32)
        if h < HEADS:
            high, low = split_query(qt[h * HEAD : (h + 1) * HEAD, :])
            query = pair_query(high, low, h % 2 == 1)
        for i in range(3):
            if h < HEADS and i < 2:
                largest = score_step((keys, keys2)[i][h // 2], query, to, pl.ds(i * HALF, HALF), largest)
            if h > 0 and i > 0:
                rows = pl.ds((i - 1) * HALF, HALF)
                o = o + weight_step((values, values2)[i - 1][h - 1], frm, rows, m)
        if h > 0:
            dt[(h - 1) * HEAD : h * HEAD, :] = o[0:HEAD, :] / o[HEAD : HEAD + 1, :]
        if h < HEADS:
            m = jnp.max(largest, axis=0, keepdims=True)
    decoded = dt[...].T.astype(BF)
    mid = x[...].astype(F32) + mm(decoded, wo[...])
    ready = norm(mid).astype(BF)
    result = hidden_layer(ready, wup, wdown, jnp.zeros((QUARTER, C), F32), 512)
    cut = pl.ds(pl.multiple_of(lax.axis_index("x") * QUARTER, QUARTER), QUARTER)
    usable = jnp.where(valid[:, cut] > 0, 1.0, 0.0).astype(F32)
    marks = jnp.concatenate([usable, jnp.zeros((7, QUARTER), F32)], 0).T
    out[...] = jnp.where(jnp.broadcast_to(marks[:, 0:1], (QUARTER, C)) > 0.5, result, 0.0)


def decode(x, qt, valid, keys, values, lb, wk, wv, wo, wup, wdown):
    vm = pl.BlockSpec(memory_space=pltpu.VMEM)
    return pl.pallas_call(
        decode_kernel,
        name="decode",
        out_shape=jax.ShapeDtypeStruct((QUARTER, C), F32),
        in_specs=[vm] * 11,
        out_specs=vm,
        scratch_shapes=[
            pltpu.VMEM(KEYS, BF),
            pltpu.VMEM(VALUES, BF),
            pltpu.VMEM((L, QUARTER), F32),
            pltpu.VMEM((L, QUARTER), F32),
            pltpu.VMEM((D, QUARTER), F32),
        ],
        compiler_params=pltpu.CompilerParams(vmem_limit_bytes=VMEM_LIMIT),
    )(x, qt, valid, keys, values, lb, wk, wv, wo, wup, wdown)


def per_device(
    tokens,
    date_index,
    valid,
    date_table,
    latents,
    wq_enc,
    wk_enc,
    wv_enc,
    wo_enc,
    w_lat_up,
    w_lat_down,
    wq_dec,
    wk_dec,
    wv_dec,
    wo_dec,
    w_out_up,
    w_out_down,
):
    date = date_index.reshape(1, TOK)
    flag = valid.reshape(1, TOK)
    swap = [(0, 1), (1, 0)]
    keep, send = encode(tokens, date, flag, date_table, latents, wq_enc, wk_enc, wv_enc)
    other = lax.ppermute(send, "c", swap)
    chunks = join_pair(keep, other)
    got = lax.all_to_all(chunks, ("z", "y"), 0, 0)
    copies = join_plane(got)
    attended = lax.all_to_all(copies, ("z", "x", "y"), 0, 0).reshape(4, 4, HALF // 4, 128)
    own = latent(attended, latents, wo_enc, w_lat_up, w_lat_down)
    others = lax.ppermute(own, "c", swap)
    x, queries = ask(tokens, date, date_table, wq_dec)
    keys, values = half(own, wk_dec, wv_dec)
    return decode(x, queries, flag, keys, values, others, wk_dec, wv_dec, wo_dec, w_out_up, w_out_down)


def solution(mesh):
    parts = Mesh(mesh.devices.reshape(4, 4, 4, 2), ("x", "y", "z", "c"))
    tok = ("y", "z", "c")
    in_specs = (
        P(tok, None),
        P(tok),
        P(tok),
        P(),
        P(),
        P(None, "x"),
        P(None, "x"),
        P(None, "x"),
        P(),
        P(),
        P(),
        P(),
        P(),
        P(),
        P(),
        P(),
        P(),
    )
    out_specs = P((*tok, "x"), None)
    return jax.shard_map(
        per_device, mesh=parts, in_specs=in_specs, out_specs=out_specs, check_vma=False
    )
```

```python
import functools

import jax
import jax.numpy as jnp
from jax import lax
from jax.experimental import pallas as pl
from jax.experimental.pallas import tpu as pltpu
from jax.sharding import Mesh, PartitionSpec as P

D = 512
HEADS = 8
HEAD = 64
L = 1024
HALF = 512
TOK = 2048
QUARTER = 512
F = 2048
C = 128
SCALE = HEAD ** (-0.5)
LOG2E = 1.4426950408889634
PAY = HALF + 8
CHUNK = 40
BF = jnp.bfloat16
F32 = jnp.float32
VMEM_LIMIT = 20 * 1024 * 1024
JOIN_LIMIT = 8 * 1024 * 1024


def mm(a, b):
    return jnp.dot(a, b, preferred_element_type=F32)


def row_pick(row, shape):
    return jnp.where(lax.broadcasted_iota(jnp.int32, shape, 0) == row, 1.0, 0.0).astype(F32)


EC = 512
EB = 256
ES = 512
ONES = 16


def hbm(*arrays):
    return [pltpu.with_memory_space_constraint(a, pltpu.HBM) for a in arrays]


def fetch(pairs, sems):
    copies = [pltpu.make_async_copy(a, b, sems.at[i]) for i, (a, b) in enumerate(pairs)]
    for copy in copies:
        copy.start()
    return copies


def split_query(q):
    scaled = q.astype(F32) * (SCALE * LOG2E)
    high = scaled.astype(BF)
    return high, (scaled - high.astype(F32)).astype(BF)


def pair_query(high, low, odd):
    zero = jnp.zeros(high.shape, BF)
    rows = [zero, high, zero, low] if odd else [high, zero, low, zero]
    return jnp.concatenate(rows, 0)


def score_step(keys, query, to, rows, largest):
    s = mm(jnp.concatenate([keys, keys], 1), query)
    to[rows, :] = s
    return jnp.maximum(largest, jnp.max(s.reshape(s.shape[0] // 8, 8, s.shape[1]), axis=0))


def weight_step(values, frm, rows, m):
    return mm(values, jnp.exp2(frm[rows, :] - m).astype(BF))


def encode_kernel(
    tok_h, date_h, valid_h, table_h, lat_h, wq_h, wk_h, wv_h, keep, send,
    tok, date, valid, table, lat, wq, wkv, kbuf, vt, qbuf, s0, s1, sems,
):
    c = lax.axis_index("c")
    pairs = [(wq_h, wq), (lat_h, lat), (date_h, date), (valid_h, valid), (table_h, table)]
    pairs += [(wk_h, wkv.at[:, 0:128]), (wv_h, wkv.at[:, 128:256])]
    pairs += [(tok_h.at[pl.ds(i * EC, EC)], tok.at[pl.ds(i * EC, EC)]) for i in range(TOK // EC)]
    copies = fetch(pairs, sems)
    copies[0].wait()
    copies[1].wait()
    for half in range(2):
        start = pl.multiple_of((1 - c if half == 0 else c) * HALF, HALF)
        q = mm(lat[pl.ds(start, HALF), :], wq[...]).astype(BF).astype(F32)
        qt = q.T.astype(BF)
        for j in range(HALF // EB):
            high, low = split_query(qt[:, j * EB : (j + 1) * EB])
            for h in range(2):
                own = slice(h * HEAD, (h + 1) * HEAD)
                qbuf[(half * 2 + j) * 2 + h] = pair_query(high[own], low[own], h == 1)
    for copy in copies[2:]:
        copy.wait()
    usable = jnp.where(valid[...] > 0, 1.0, 0.0).astype(F32)
    second = jnp.where(date[...] == 1, 1.0, 0.0).astype(F32)
    flags = jnp.concatenate([second, usable, jnp.zeros((6, TOK), F32)], 0)
    row0, row1 = table[0:1, :], table[1:2, :]
    for h in range(2):
        vt[h, HEAD : HEAD + ONES, :] = jnp.concatenate([usable, jnp.zeros((ONES - 1, TOK), F32)], 0).astype(BF)
    for i in range(TOK // EC):
        rows = pl.ds(i * EC, EC)
        cols = slice(i * EC, (i + 1) * EC)
        marks = flags[:, cols].T
        shift = jnp.where(jnp.broadcast_to(marks[:, 0:1], (EC, D)) > 0.5, row1, row0)
        x = (tok[rows, :].astype(F32) + shift).astype(BF)
        kv = mm(x, wkv[...])
        k = kv[:, 0:128]
        first = jnp.broadcast_to(k.reshape(EC // 16, 16, 128)[:, 0:1, :], (EC // 16, 16, 128)).reshape(EC, 128)
        kbuf[rows, :] = jnp.where(jnp.broadcast_to(marks[:, 1:2], (EC, 128)) > 0.5, k, first).astype(BF)
        v = (kv[:, 128:256].astype(BF).astype(F32).T * usable[:, cols]).astype(BF)
        vt[0, 0:HEAD, cols] = v[0:HEAD]
        vt[1, 0:HEAD, cols] = v[HEAD:128]

    low_start = jnp.full((8, EB), -jnp.inf, F32)
    blocks = 2 * L // EB

    def step(n, frm, to, m, odd, score, weigh):
        largest = low_start
        o = jnp.zeros((HEAD + ONES, EB), F32)
        for i in range(TOK // ES):
            rows = pl.ds(i * ES, ES)
            if score:
                largest = score_step(kbuf[rows, :], qbuf[n + 1], to, rows, largest)
            if weigh:
                o = o + weight_step(vt[odd, :, i * ES : (i + 1) * ES], frm, rows, m)
        t = o[HEAD : HEAD + 1, :]
        return jnp.max(largest, axis=0, keepdims=True), o[0:HEAD, :] / t if weigh else None, m + jnp.log2(t)

    def put(to, j, o0, o1, l0, l1):
        to[pl.ds(pl.multiple_of(j * EB, EB), EB), :] = jnp.concatenate([o0, o1], 0).T
        for h, line in enumerate((l0, l1)):
            for k in range(EB // 128):
                to[pl.ds(HALF + h * 4 + j * (EB // 128) + k, 1), :] = line[:, k * 128 : (k + 1) * 128]

    m, _, _ = step(-1, s1, s0, jnp.zeros((1, EB), F32), 0, True, False)
    for j in range(L // EB):
        to = send if j < HALF // EB else keep
        m, o0, l0 = step(2 * j, s0, s1, m, 0, True, True)
        m, o1, l1 = step(2 * j + 1, s1, s0, m, 1, j < L // EB - 1, True)
        put(to, j % (HALF // EB), o0, o1, l0, l1)


def encode(tok, date, valid, table, lat, wq, wk, wv):
    blocks = 2 * L // EB
    vm = pl.BlockSpec(memory_space=pltpu.VMEM)
    return pl.pallas_call(
        encode_kernel,
        name="encode",
        out_shape=(jax.ShapeDtypeStruct((PAY, 128), F32),) * 2,
        in_specs=[pl.BlockSpec(memory_space=pltpu.HBM)] * 8,
        out_specs=(vm, vm),
        scratch_shapes=[
            pltpu.VMEM((TOK, D), BF),
            pltpu.VMEM((1, TOK), jnp.int32),
            pltpu.VMEM((1, TOK), jnp.int32),
            pltpu.VMEM((2, D), F32),
            pltpu.VMEM((L, D), BF),
            pltpu.VMEM((D, 128), BF),
            pltpu.VMEM((D, 256), BF),
            pltpu.VMEM((TOK, 128), BF),
            pltpu.VMEM((2, HEAD + ONES, TOK), BF),
            pltpu.VMEM((blocks, 256, EB), BF),
            pltpu.VMEM((TOK, EB), F32),
            pltpu.VMEM((TOK, EB), F32),
            pltpu.SemaphoreType.DMA((7 + TOK // EC,)),
        ],
        compiler_params=pltpu.CompilerParams(vmem_limit_bytes=VMEM_LIMIT),
        cost_estimate=pl.CostEstimate(
            flops=2 * TOK * D * 256 + 4 * 2 * L * TOK * HEAD + 2 * L * D * 128,
            bytes_accessed=4 << 20,
            transcendentals=2 * L * TOK,
        ),
    )(*hbm(tok, date, valid, table, lat, wq, wk, wv))


def join_pair_kernel(mine, theirs, out):
    a, b = mine[HALF:PAY, :], theirs[HALF:PAY, :]
    top = jnp.maximum(a, b)
    ea, eb = jnp.exp2(a - top), jnp.exp2(b - top)
    total = ea + eb
    lse = top + jnp.log2(total)
    wa, wb = (ea / total).T, (eb / total).T
    left = lax.broadcasted_iota(jnp.int32, (128, 128), 1) < HEAD
    for t in range(4):
        fa = jnp.where(left, wa[:, t : t + 1], wa[:, 4 + t : 5 + t])
        fb = jnp.where(left, wb[:, t : t + 1], wb[:, 4 + t : 5 + t])
        rows = pl.ds(t * 128, 128)
        o = mine[rows, :] * fa + theirs[rows, :] * fb
        for k in range(4):
            out[t * 4 + k, 0:32, :] = o[k * 32 : (k + 1) * 32, :]
            out[t * 4 + k, 32:40, :] = jnp.concatenate(
                [lse[t : t + 1, :], lse[4 + t : 5 + t, :], jnp.zeros((6, 128), F32)], 0
            )


def join_pair(mine, theirs):
    return pl.pallas_call(
        join_pair_kernel,
        name="join_pair",
        out_shape=jax.ShapeDtypeStruct((16, CHUNK, 128), F32),
        in_specs=[pl.BlockSpec(memory_space=pltpu.VMEM)] * 2,
        out_specs=pl.BlockSpec(memory_space=pltpu.VMEM),
        compiler_params=pltpu.CompilerParams(vmem_limit_bytes=JOIN_LIMIT),
    )(mine, theirs)


def join_plane_kernel(got, out, turned):
    rows = jnp.concatenate([got[s, 32:33, :] for s in range(16)] + [got[s, 33:34, :] for s in range(16)], 0)
    weights = []
    for h in range(2):
        part = rows[h * 16 : (h + 1) * 16, :]
        top = jnp.max(part, axis=0, keepdims=True)
        e = jnp.exp2(part - top)
        weights.append(e / jnp.sum(e, axis=0, keepdims=True))
    turned[:, 0:32] = jnp.concatenate(weights, 0).T
    start = pl.multiple_of(lax.axis_index("y") * 32, 32)
    cols = turned[pl.ds(start, 32), :]
    left = lax.broadcasted_iota(jnp.int32, (32, 128), 1) < HEAD
    o = jnp.zeros((32, 128), F32)
    for s in range(16):
        o = o + got[s, 0:32, :] * jnp.where(left, cols[:, s : s + 1], cols[:, 16 + s : 17 + s])
    out[...] = jnp.broadcast_to(o.astype(BF)[None], (64, 32, 128))


def join_plane(got):
    return pl.pallas_call(
        join_plane_kernel,
        name="join_plane",
        out_shape=jax.ShapeDtypeStruct((64, 32, 128), BF),
        in_specs=[pl.BlockSpec(memory_space=pltpu.VMEM)],
        out_specs=pl.BlockSpec(memory_space=pltpu.VMEM),
        scratch_shapes=[pltpu.VMEM((128, 128), F32)],
        compiler_params=pltpu.CompilerParams(vmem_limit_bytes=JOIN_LIMIT),
    )(got)


def norm(v):
    center = v - jnp.mean(v, axis=-1, keepdims=True)
    spread = jnp.mean(center * center, axis=-1, keepdims=True)
    return center * lax.rsqrt(spread + 1e-05)


def gelu(v):
    half = 0.5 * v
    return half + half * jnp.tanh(v * (0.7978845608028654 + 0.03567740813636141 * (v * v)))


def hidden_layer(ready, wup, wdown, total, width):
    for i in range(F // width):
        cut = slice(i * width, (i + 1) * width)
        total = total + mm(gelu(mm(ready, wup[:, cut])).astype(BF), wdown[cut, :])
    return total


def latent_kernel(att, lat, wo, wup, wdown, out):
    start = pl.multiple_of(lax.axis_index("c") * HALF, HALF)
    a = jnp.concatenate([jnp.concatenate([att[z, x] for z in range(4)], 0) for x in range(4)], 1)
    mid = lat[pl.ds(start, HALF), :].astype(F32) + mm(a, wo[...])
    out[...] = hidden_layer(norm(mid).astype(BF), wup, wdown, mid, 256).astype(BF)


def latent(att, lat, wo, wup, wdown):
    vm = pl.BlockSpec(memory_space=pltpu.VMEM)
    return pl.pallas_call(
        latent_kernel,
        name="latent",
        out_shape=jax.ShapeDtypeStruct((HALF, D), BF),
        in_specs=[vm] * 5,
        out_specs=vm,
        compiler_params=pltpu.CompilerParams(vmem_limit_bytes=VMEM_LIMIT),
    )(att, lat, wo, wup, wdown)


def ask_kernel(tok, date, table, wq, x, qt):
    cut = pl.ds(pl.multiple_of(lax.axis_index("x") * QUARTER, QUARTER), QUARTER)
    second = jnp.where(date[:, cut] == 1, 1.0, 0.0).astype(F32)
    marks = jnp.concatenate([second, jnp.zeros((7, QUARTER), F32)], 0).T
    shift = jnp.where(jnp.broadcast_to(marks[:, 0:1], (QUARTER, D)) > 0.5, table[1:2, :], table[0:1, :])
    own = (tok[cut, :].astype(F32) + shift).astype(BF)
    x[...] = own
    high, low = split_query(mm(own, wq[...]).astype(BF).astype(F32).T.astype(BF))
    for h in range(HEADS):
        rows = slice(h * HEAD, (h + 1) * HEAD)
        qt[h] = pair_query(high[rows], low[rows], h % 2 == 1)


def ask(tok, date, table, wq):
    vm = pl.BlockSpec(memory_space=pltpu.VMEM)
    return pl.pallas_call(
        ask_kernel,
        name="ask",
        out_shape=(jax.ShapeDtypeStruct((QUARTER, D), BF), jax.ShapeDtypeStruct((HEADS, 4 * HEAD, QUARTER), BF)),
        in_specs=[vm] * 4,
        out_specs=(vm, vm),
        compiler_params=pltpu.CompilerParams(vmem_limit_bytes=JOIN_LIMIT),
        cost_estimate=pl.CostEstimate(flops=2 * QUARTER * D * D, bytes_accessed=2 << 20, transcendentals=0),
    )(tok, date, table, wq)


def half_kernel(latents, wk, wv, keys, values):
    k = mm(latents[...], wk[...]).astype(BF)
    for pair in range(HEADS // 2):
        keys[pair] = k[:, pair * 128 : (pair + 1) * 128]
    v = mm(latents[...], wv[...]).astype(BF).astype(F32).T.astype(BF)
    ones = row_pick(0, (ONES, HALF)).astype(BF)
    for h in range(HEADS):
        values[h] = jnp.concatenate([v[h * HEAD : (h + 1) * HEAD], ones], 0)


KEYS = (HEADS // 2, HALF, 128)
VALUES = (HEADS, HEAD + ONES, HALF)


def half(latents, wk, wv):
    vm = pl.BlockSpec(memory_space=pltpu.VMEM)
    return pl.pallas_call(
        half_kernel,
        name="half",
        out_shape=(jax.ShapeDtypeStruct(KEYS, BF), jax.ShapeDtypeStruct(VALUES, BF)),
        in_specs=[vm] * 3,
        out_specs=(vm, vm),
        compiler_params=pltpu.CompilerParams(vmem_limit_bytes=JOIN_LIMIT),
        cost_estimate=pl.CostEstimate(flops=4 * HALF * D * D, bytes_accessed=3 << 20, transcendentals=0),
    )(latents, wk, wv)


def decode_kernel(x, qt, valid, keys, values, lb, wk, wv, wo, wup, wdown, out, keys2, values2, s0, s1, dt):
    half_kernel(lb, wk, wv, keys2, values2)
    low_start = jnp.full((8, QUARTER), -jnp.inf, F32)
    m = None
    for h in range(HEADS + 1):
        to, frm = (s0, s1) if h % 2 == 0 else (s1, s0)
        largest = low_start
        o = jnp.zeros((HEAD + ONES, QUARTER), F32)
        if h < HEADS:
            query = qt[h]
        for i in range(3):
            if h < HEADS and i < 2:
                largest = score_step((keys, keys2)[i][h // 2], query, to, pl.ds(i * HALF, HALF), largest)
            if h > 0 and i > 0:
                rows = pl.ds((i - 1) * HALF, HALF)
                o = o + weight_step((values, values2)[i - 1][h - 1], frm, rows, m)
        if h > 0:
            dt[(h - 1) * HEAD : h * HEAD, :] = o[0:HEAD, :] / o[HEAD : HEAD + 1, :]
        if h < HEADS:
            m = jnp.max(largest, axis=0, keepdims=True)
    decoded = dt[...].T.astype(BF)
    mid = x[...].astype(F32) + mm(decoded, wo[...])
    ready = norm(mid).astype(BF)
    result = hidden_layer(ready, wup, wdown, jnp.zeros((QUARTER, C), F32), 512)
    cut = pl.ds(pl.multiple_of(lax.axis_index("x") * QUARTER, QUARTER), QUARTER)
    usable = jnp.where(valid[:, cut] > 0, 1.0, 0.0).astype(F32)
    marks = jnp.concatenate([usable, jnp.zeros((7, QUARTER), F32)], 0).T
    out[...] = jnp.where(jnp.broadcast_to(marks[:, 0:1], (QUARTER, C)) > 0.5, result, 0.0)


def decode(x, qt, valid, keys, values, lb, wk, wv, wo, wup, wdown):
    vm = pl.BlockSpec(memory_space=pltpu.VMEM)
    return pl.pallas_call(
        decode_kernel,
        name="decode",
        out_shape=jax.ShapeDtypeStruct((QUARTER, C), F32),
        in_specs=[vm] * 11,
        out_specs=vm,
        scratch_shapes=[
            pltpu.VMEM(KEYS, BF),
            pltpu.VMEM(VALUES, BF),
            pltpu.VMEM((L, QUARTER), F32),
            pltpu.VMEM((L, QUARTER), F32),
            pltpu.VMEM((D, QUARTER), F32),
        ],
        compiler_params=pltpu.CompilerParams(vmem_limit_bytes=VMEM_LIMIT),
    )(x, qt, valid, keys, values, lb, wk, wv, wo, wup, wdown)


def per_device(
    tokens,
    date_index,
    valid,
    date_table,
    latents,
    wq_enc,
    wk_enc,
    wv_enc,
    wo_enc,
    w_lat_up,
    w_lat_down,
    wq_dec,
    wk_dec,
    wv_dec,
    wo_dec,
    w_out_up,
    w_out_down,
):
    date = date_index.reshape(1, TOK)
    flag = valid.reshape(1, TOK)
    swap = [(0, 1), (1, 0)]
    keep, send = encode(tokens, date, flag, date_table, latents, wq_enc, wk_enc, wv_enc)
    other = lax.ppermute(send, "c", swap)
    chunks = join_pair(keep, other)
    got = lax.all_to_all(chunks, ("z", "y"), 0, 0)
    copies = join_plane(got)
    attended = lax.all_to_all(copies, ("z", "x", "y"), 0, 0).reshape(4, 4, HALF // 4, 128)
    own = latent(attended, latents, wo_enc, w_lat_up, w_lat_down)
    others = lax.ppermute(own, "c", swap)
    x, queries = ask(tokens, date, date_table, wq_dec)
    keys, values = half(own, wk_dec, wv_dec)
    return decode(x, queries, flag, keys, values, others, wk_dec, wv_dec, wo_dec, w_out_up, w_out_down)


def solution(mesh):
    parts = Mesh(mesh.devices.reshape(4, 4, 4, 2), ("x", "y", "z", "c"))
    tok = ("y", "z", "c")
    in_specs = (
        P(tok, None),
        P(tok),
        P(tok),
        P(),
        P(),
        P(None, "x"),
        P(None, "x"),
        P(None, "x"),
        P(),
        P(),
        P(),
        P(),
        P(),
        P(),
        P(),
        P(),
        P(),
    )
    out_specs = P((*tok, "x"), None)
    return jax.shard_map(
        per_device, mesh=parts, in_specs=in_specs, out_specs=out_specs, check_vma=False
    )
```
